32 devices in a mesh: gx: 4 (over z), gy: 8 (over y, x, core).
Axes of the slice: x: 2, y: 2, z: 4, core: 2. Of those that a mesh axis runs over, the one named last changes fastest.
Arguments:
- multipoles: float32 [56, 40960], P(None, ('gx', 'gy')), may hold values from -6 to 6
- trans: float32 [316, 56, 56], replicated, may hold values from -0.078125 to 0.078125
- pair_target: int32 [316, 8192], P(None, ('gx', 'gy')), may hold values from -1 to 1279, as said below
- pair_source: int32 [316, 8192], P(None, ('gx', 'gy')), may hold values from -1 to 2815, as said below
- send_list: int32 [32, 1536], P(('gx', 'gy')), may hold values from 0 to 1279
Outputs:
- locals_out: float32 [56, 40960], P(None, ('gx', 'gy'))
The draws below stay inside these ranges and needn't reach their ends.
Inputs may be any that keep to these rules, and one draw needn't show every extreme that they name: `pair_target`: in each offset, the used slots of a device come first; in every offset some device uses all 256 slots. Unused slots hold -1 in both lists. `pair_source`: -1 exactly where pair_target is -1. A position past 1280 lies among the first entries of its block, up to a live count of that block which differs from device to device and block to block (from zero to 128; zero for the block from the device itself and for neighbours past either end of gy; 128 for some block of every device).
All inputs are finite; a program needn't handle non-finite values.
Results may differ from the reference program's by a relative error of at most 0.0003.
Values sent between devices are 32-bit elements; how exact they have to be, the bound alone decides.
No kernel may reach another device: no remote copies, remote signals or barrier semaphores. Data moves between devices by JAX's collectives and lax.ppermute only.
A program may use at most 128 MiB of HBM per device.

```python
import jax
import jax.numpy as jnp
from jax import lax

TERMS = 56
OFFSETS = 316
REACH = 4
CELLS_DEV = 1280
SLOTS = 256
HALO = 128
NEAR = 12
PEERS = 32
CELLS = 40960
N_GX = 4
N_GY = 8


def slot_usable(key):
    key_level, key_count, key_full = jax.random.split(jax.random.fold_in(key, 11), 3)
    device_level = jax.random.randint(key_level, (PEERS,), 1, 5)
    ceiling = SLOTS * device_level // 4
    drawn = jax.random.randint(key_count, (OFFSETS, PEERS), 0, 1 << 20) % (ceiling + 1)[None, :]
    fullest = jax.random.randint(key_full, (OFFSETS,), 0, PEERS)
    fullest = fullest.at[0].set(0)
    counts = jnp.where(jnp.arange(PEERS)[None, :] == fullest[:, None], SLOTS, drawn)
    counts = counts.at[0, REACH].set(SLOTS)
    counts = counts.at[0, PEERS - 1].set(0)
    position = jnp.arange(SLOTS)
    usable = position[None, None, :] < counts[:, :, None]
    return usable.reshape(OFFSETS, PEERS * SLOTS)


def live_counts(key):
    key_outer, key_upper, key_lower, key_full = jax.random.split(jax.random.fold_in(key, 17), 4)
    devices = jnp.arange(PEERS)
    outer_here = devices // N_GY
    inner_here = devices % N_GY
    lowest = max(1, HALO // 4)
    outer = jax.random.randint(key_outer, (PEERS, N_GX), lowest, HALO + 1)
    outer = jnp.where(jnp.arange(N_GX)[None, :] == outer_here[:, None], 0, outer)
    fullest = (outer_here + 1 + jax.random.randint(key_full, (PEERS,), 0, N_GX - 1)) % N_GX
    outer = jnp.where(jnp.arange(N_GX)[None, :] == fullest[:, None], HALO, outer)
    steps_up = jnp.arange(1, REACH + 1)
    floor_count = jnp.where(steps_up == 1, lowest, 0)
    upper = floor_count[None, :] + jax.random.randint(key_upper, (PEERS, REACH), 0, 1 << 20) % (HALO + 1 - floor_count)[None, :]
    upper = jnp.where(inner_here[:, None] + steps_up[None, :] < N_GY, upper, 0)
    upper = upper.at[0, REACH - 1].set(HALO)
    lower = floor_count[None, :] + jax.random.randint(key_lower, (PEERS, REACH), 0, 1 << 20) % (HALO + 1 - floor_count)[None, :]
    lower = jnp.where(inner_here[:, None] - steps_up[None, :] >= 0, lower, 0)
    lower = lower.at[REACH, REACH - 1].set(HALO)
    return jnp.concatenate([outer, upper, lower], axis=1)


def draw_pair_target(key, part):
    usable = slot_usable(key)
    key = jax.random.fold_in(key, 3)
    picks = jax.random.randint(key, (OFFSETS, PEERS * SLOTS), 0, CELLS_DEV)
    picks = picks.at[0, 0].set(CELLS_DEV - 1)
    return jnp.where(usable, picks, -1).astype(jnp.int32)


def draw_pair_source(key, part):
    usable = slot_usable(key)
    counts = live_counts(key)
    key = jax.random.fold_in(key, 5)
    key_local, key_block, key_within, key_side = jax.random.split(key, 4)
    shape = (OFFSETS, PEERS * SLOTS)
    owners = jnp.arange(PEERS * SLOTS) // SLOTS
    local_pick = jax.random.randint(key_local, shape, 0, CELLS_DEV)
    block_pick = jax.random.randint(key_block, shape, 0, NEAR)
    live = counts[jnp.broadcast_to(owners[None, :], shape), block_pick]
    within = jax.random.randint(key_within, shape, 0, 1 << 20) % jnp.maximum(live, 1)
    ghost_pick = CELLS_DEV + block_pick * HALO + within
    choose_ghost = (jax.random.randint(key_side, shape, 0, 2) == 0) & (live > 0)
    picked = jnp.where(choose_ghost, ghost_pick, local_pick)
    picked = picked.at[0, REACH * SLOTS].set(CELLS_DEV + NEAR * HALO - 1)
    return jnp.where(usable, picked, -1).astype(jnp.int32)


def touch_ends(values, own_key, least, largest):
    extent = values.shape
    spot = [jax.random.randint(jax.random.fold_in(own_key, axis), (), 0, extent[axis]) for axis in range(len(extent))]
    values = values.at[tuple(spot)].set(least)
    longest = extent.index(max(extent))
    spot[longest] = (spot[longest] + 1) % extent[longest]
    return values.at[tuple(spot)].set(largest)


def block_levels(stream_key, dims, cuts, least, largest):
    loudness, own = 1.0, jax.random.fold_in(stream_key, 6)
    for dim, parts in cuts:
        draws = jnp.exp(jax.random.uniform(jax.random.fold_in(own, dim), (parts,), jnp.float32, least / len(cuts), largest / len(cuts)))
        loudness = loudness * jnp.repeat(draws, dims[dim] // parts).reshape([-1 if axis == dim else 1 for axis in range(len(dims))])
    return loudness


def centred(key, dims, scale, reach, shards=(), kind=jnp.bfloat16):
    result = jax.random.normal(key, dims, jnp.float32) * scale
    if len(shards) > 0:
        result = block_levels(key, dims, shards, -0.22, 0.18) * result
    return jnp.clip(result, min=-reach, max=reach).astype(kind)


def setup_inputs(seed: int = 0) -> dict:
    seeds = jax.random.split(jax.random.key(seed), 6)
    multipoles = centred(seeds[0], (TERMS, CELLS), 1.0, 6.0, ((1, 32),), jnp.float32)
    trans = centred(seeds[1], (OFFSETS, TERMS, TERMS), (TERMS * 100) ** -0.5, 0.078125, (), jnp.float32)
    pair_target = draw_pair_target(jax.random.fold_in(seeds[5], 71), 0)
    pair_source = draw_pair_source(jax.random.fold_in(seeds[5], 71), 0)
    send_list = touch_ends(jax.random.randint(seeds[4], (PEERS, NEAR * HALO), 0, CELLS_DEV), jax.random.fold_in(seeds[4], 1), 0, CELLS_DEV - 1).astype(jnp.int32)
    return dict(multipoles=multipoles, trans=trans, pair_target=pair_target, pair_source=pair_source, send_list=send_list)


def parity_signs():
    term_index = jnp.arange(TERMS, dtype=jnp.int32)
    degree = (term_index >= 1).astype(jnp.int32) + (term_index >= 4).astype(jnp.int32)
    degree = degree + (term_index >= 10).astype(jnp.int32) + (term_index >= 20).astype(jnp.int32)
    degree = degree + (term_index >= 35).astype(jnp.int32)
    return jnp.where(degree % 2 == 0, 1.0, -1.0).astype(jnp.float32)


def ghost_table(send_list):
    devices = jnp.arange(PEERS, dtype=jnp.int32)
    outer_here = devices // N_GY
    inner_here = devices % N_GY
    outer_src = jnp.arange(N_GX, dtype=jnp.int32)[None, :] * N_GY + inner_here[:, None]
    outer_col = jnp.broadcast_to((outer_here * HALO)[:, None], (PEERS, N_GX))
    steps_up = jnp.arange(1, REACH + 1, dtype=jnp.int32)
    upper_src = jnp.minimum(devices[:, None] + steps_up[None, :], PEERS - 1)
    upper_col = jnp.broadcast_to(((N_GX + steps_up - 1) * HALO)[None, :], (PEERS, REACH))
    lower_src = jnp.maximum(devices[:, None] - steps_up[None, :], 0)
    lower_col = jnp.broadcast_to(((N_GX + REACH + steps_up - 1) * HALO)[None, :], (PEERS, REACH))
    source_dev = jnp.concatenate([outer_src, upper_src, lower_src], axis=1).astype(jnp.int32)
    base_col = jnp.concatenate([outer_col, upper_col, lower_col], axis=1).astype(jnp.int32)
    within = jnp.arange(HALO, dtype=jnp.int32)
    cols = base_col[:, :, None] + within[None, None, :]
    rows = jnp.broadcast_to(source_dev[:, :, None], cols.shape)
    cells = send_list[rows, cols] + rows * CELLS_DEV
    return cells.reshape(PEERS, NEAR * HALO).astype(jnp.int32)


def reference(multipoles, trans, pair_target, pair_source, send_list):
    parity = parity_signs()[:, None]
    ghost_cells = ghost_table(send_list)
    owners = (jnp.arange(PEERS * SLOTS, dtype=jnp.int32) // SLOTS).astype(jnp.int32)

    def one_offset(totals, pieces):
        matrix, target, source = pieces
        usable = (target >= 0).astype(jnp.float32)[None, :]
        target_ids = owners * CELLS_DEV + jnp.maximum(target, 0)
        ghost_pos = jnp.clip(source - CELLS_DEV, 0, NEAR * HALO - 1)
        source_ids = jnp.where(source < CELLS_DEV, owners * CELLS_DEV + jnp.maximum(source, 0), ghost_cells[owners, ghost_pos])
        source_cols = multipoles[:, source_ids]
        target_cols = multipoles[:, target_ids]
        forward = jnp.dot(matrix, source_cols, precision=lax.Precision.HIGHEST) * usable
        backward = parity * jnp.dot(matrix, parity * target_cols, precision=lax.Precision.HIGHEST) * usable
        totals = totals.at[:, target_ids].add(forward)
        totals = totals.at[:, source_ids].add(backward)
        return totals, None

    start = jnp.zeros((TERMS, CELLS_DEV * PEERS), jnp.float32)
    totals, _ = lax.scan(one_offset, start, (trans, pair_target, pair_source))
    return totals
```

```python
import functools

import jax
import jax.numpy as jnp
from jax import lax
from jax.experimental import pallas as pl
from jax.experimental.pallas import tpu as pltpu
from jax.sharding import PartitionSpec as P

REACH = 4
LANES = 128
SUBLANES = 16
WIDTH = 1024
GRAIN = 32
FOLD = 256
SCRATCHES = 14
SHORT = 64
PACK_LIMIT = 60 * 1024 * 1024
VMEM_LIMIT = 53 * 1024 * 1024
SMALL_LIMIT = 16 * 1024 * 1024


def parity_signs(term_count):
    term_index = jnp.arange(term_count, dtype=jnp.int32)
    degree = (term_index >= 1).astype(jnp.int32) + (term_index >= 4).astype(jnp.int32)
    degree = degree + (term_index >= 10).astype(jnp.int32) + (term_index >= 20).astype(jnp.int32)
    degree = degree + (term_index >= 35).astype(jnp.int32)
    return jnp.where(degree % 2 == 0, 1.0, -1.0).astype(jnp.float32)


def hot_columns(places, size):
    count = places[0].shape[1]
    tall = (SUBLANES, count)
    one, none = jnp.ones((), jnp.bfloat16), jnp.zeros((), jnp.bfloat16)
    row = lax.broadcasted_iota(jnp.int32, tall, 0).astype(jnp.float32)
    rows = [(row + float(k)).astype(jnp.bfloat16) for k in range(0, size, SUBLANES)]
    blocks = []
    for place in places:
        wanted = jnp.broadcast_to(place.astype(jnp.float32), tall).astype(jnp.bfloat16)
        blocks += [jnp.where(one_row == wanted, one, none) for one_row in rows]
    return jnp.concatenate(blocks, axis=0)


def stack_parts(values):
    high = values.astype(jnp.bfloat16).astype(jnp.float32)
    return jnp.concatenate([high, values - high], axis=0).astype(jnp.bfloat16)


def scatter_product(index_row, half, parts):
    rows, count = parts.shape
    upper = jnp.broadcast_to(index_row >= half, (rows, count))
    none = jnp.zeros((), jnp.bfloat16)
    pad = jnp.zeros((LANES - rows, count), jnp.bfloat16)
    spread = jnp.concatenate([jnp.where(upper, none, parts), pad, jnp.where(upper, parts, none), pad], axis=0)
    place = jnp.where(index_row >= half, index_row - half, index_row)
    hot = hot_columns([place - j * LANES for j in range(half // LANES)], LANES)
    return lax.dot_general(
        hot, spread, (((1,), (1,)), ((), ())), preferred_element_type=jnp.float32
    )


def unfold(acc_ref, terms):
    sides = []
    for side in range(2):
        turned = acc_ref[:, side * LANES : (side + 1) * LANES].T
        sides.append(turned[:terms] + turned[terms : 2 * terms])
    return jnp.concatenate(sides, axis=1)


def pick(options, which):
    chosen = options[0]
    for k in range(1, len(options)):
        chosen = jnp.where(which == k, options[k], chosen)
    return chosen


def batch_of(count, most):
    return max(k for k in range(1, most + 1) if count % k == 0)


def compact(starts_ref, tables):
    offset_count, slot_count = tables[0][0].shape
    pieces = slot_count // LANES
    for _, out_ref in tables:
        out_ref[...] = jnp.full(out_ref.shape, -1, jnp.int32)
    lane = lax.broadcasted_iota(jnp.int32, (8, LANES), 1)
    empty = jnp.full((8, LANES), -1, jnp.int32)
    batch = batch_of(offset_count, 4)

    def place(step, kept):
        kept = list(kept)
        for u in range(batch):
            offset = step * batch + u
            start = starts_ref[offset]
            row, shift = start >> 7, start & (LANES - 1)
            crossed = (starts_ref[offset + 1] >> 7) - row
            inside = lane >= shift
            for k, (pairs_ref, out_ref) in enumerate(tables):
                line = pairs_ref[pl.ds(offset, 1), :]
                turned = [
                    pltpu.roll(jnp.broadcast_to(line[:, q * LANES : (q + 1) * LANES], (8, LANES)), shift, 1)
                    for q in range(pieces)
                ]
                turned = [kept[k], *turned, empty]
                tiles = [jnp.where(inside, turned[q + 1], turned[q]) for q in range(pieces + 1)]
                for q, tile in enumerate(tiles):
                    out_ref[pl.ds(row + q, 1), :] = tile[:1]
                kept[k] = pick(tiles, crossed)
        return tuple(kept)

    lax.fori_loop(0, offset_count // batch, place, (empty,) * len(tables))


def turn_matrices(t_ref, matrix_ref):
    terms, _, offset_count = t_ref.shape
    turns = batch_of(terms, 4)
    pad = jnp.zeros((LANES - 2 * terms, offset_count), jnp.float32)

    def turn(step, carry):
        for u in range(turns):
            i = step * turns + u
            block = t_ref[i]
            matrix_ref[pl.ds(i, offset_count, stride=terms), :] = jnp.concatenate([block, block, pad], axis=0).T
        return carry

    lax.fori_loop(0, terms // turns, turn, 0)


def index_row(ref, first, count):
    return jnp.concatenate([ref[pl.ds(first + q, 1), :] for q in range(count)], axis=1)


def gather_columns(parts, index):
    terms = parts[0].shape[0]
    lane = jnp.broadcast_to(index & (LANES - 1), (terms, LANES))
    chunk = jnp.broadcast_to(index >> 7, (8, LANES))
    picked = [jnp.zeros((8, LANES), jnp.float32)] * (terms // 8)
    for c, part in enumerate(parts):
        found = jnp.take_along_axis(part[...], lane, axis=1, mode="promise_in_bounds")
        here = chunk == c
        picked = [jnp.where(here, found[8 * r : 8 * r + 8], some) for r, some in enumerate(picked)]
    return jnp.concatenate(picked, axis=0)


def fold_columns(fold_ref, parts, index):
    count = index.shape[1]
    hot = hot_columns([index & (FOLD - 1)], FOLD)
    found = jnp.dot(fold_ref[...], hot, preferred_element_type=jnp.float32)
    chunk = jnp.broadcast_to(index >> (FOLD.bit_length() - 1), (8, count))
    masks = [chunk == c for c in range(fold_ref.shape[0] // parts)]
    picked = []
    for r in range(0, parts, 8):
        some = jnp.zeros((8, count), jnp.float32)
        for c, mask in enumerate(masks):
            some = jnp.where(mask, found[c * parts + r : c * parts + r + 8], some)
        picked.append(some)
    return jnp.concatenate(picked, axis=0).astype(jnp.bfloat16)


def block_for(place, here, sign):
    distance = (place - here) * sign
    block = jnp.where(distance > 0, distance - 1, REACH - 1 - distance)
    there = (distance != 0) & (distance <= REACH) & (distance >= -REACH)
    return jnp.where(there, block, 0), there


def sender_of(block, here, sign, count):
    step = block + 1 if block < REACH else REACH - 1 - block
    place = here - step * sign
    return jnp.clip(place, 0, count - 1), (place >= 0) & (place < count)


def turned(place, count):
    return jnp.where(place >= count, place - count, jnp.where(place < 0, place + count, place))


def upper_blocks(here, count):
    return jnp.minimum(count - 1 - here, REACH)


def rank_of(block, here_ref, outer_count, inner_count):
    outer = block - jnp.where(block > here_ref[0], 1, 0)
    lower = block - 1 - REACH + upper_blocks(here_ref[1], inner_count)
    return jnp.where(block < outer_count, outer, jnp.where(block < outer_count + REACH, block - 1, lower))


def most_blocks(outer_count, inner_count):
    along = [min(REACH, inner_count - 1 - p) + min(REACH, p) for p in range(inner_count)]
    return outer_count - 1 + max(along)


def hand_out(read, here_ref, sign, outer_refs, inner_ref):
    outer_count = len(outer_refs) + 1
    for k, ref in enumerate(outer_refs):
        ref[...] = read(turned(here_ref[0] + k + 1, outer_count), True)

    def hand(place, carry):
        block, there = block_for(place, here_ref[1], sign)
        inner_ref[place] = read(outer_count + block, there)
        return carry

    lax.fori_loop(0, inner_ref.shape[0], hand, 0)


def take_in(put, here_ref, sign, outer_refs, inner_ref):
    outer_count = len(outer_refs) + 1
    for k, ref in enumerate(outer_refs):
        put(turned(here_ref[0] - k - 1, outer_count), True, ref[...])
    for block in range(2 * REACH):
        sender, there = sender_of(block, here_ref[1], sign, inner_ref.shape[0])
        put(outer_count + block, there, inner_ref[sender])


def translate_kernel(*refs):
    outer_count = (len(refs) - SCRATCHES - 11) // 2
    inputs, refs = refs[:9], refs[9:]
    outer_refs, refs = refs[:outer_count], refs[outer_count:]
    own_ref, inner_back_ref, refs = refs[0], refs[1], refs[2:]
    outer_back_refs, refs = refs[:outer_count], refs[outer_count:]
    translate_body(*inputs, outer_refs, own_ref, inner_back_ref, outer_back_refs, *refs)


def translate_body(
    starts_ref, offsets_ref, here_ref, pair_target_ref, pair_source_ref, trans_ref, multipoles_ref, sign_ref, inner_ref,
    outer_refs, own_ref, inner_back_ref, outer_back_refs,
    target_pairs_ref, source_pairs_ref, native_ref, x_ref, target_ref, source_ref, t_ref,
    fold_ref, near_ref, forward_ref, backward_ref, own_acc_ref, all_acc_ref, ready
):
    fetches = [
        pltpu.make_async_copy(here, there, ready.at[k])
        for k, (here, there) in enumerate(
            [
                (pair_target_ref, target_pairs_ref),
                (pair_source_ref, source_pairs_ref),
                (multipoles_ref, x_ref),
                (trans_ref, native_ref),
            ]
        )
    ]
    for fetch in fetches:
        fetch.start()
    terms, cells = x_ref.shape
    outer_count, inner_count = len(outer_refs) + 1, inner_ref.shape[0]
    spare = near_ref.shape[0] - 1
    chunks = cells // LANES
    own_half = cells // 2
    all_half = all_acc_ref.shape[0]
    parts = 2 * terms
    per_step = WIDTH // LANES
    grains = LANES // GRAIN

    for fetch in fetches[:3]:
        fetch.wait()
    folds = cells // FOLD
    for c in range(folds):
        fold_ref[c * parts : (c + 1) * parts, :] = stack_parts(x_ref[:, c * FOLD : (c + 1) * FOLD] * sign_ref[...])
    near_ref[...] = jnp.zeros_like(near_ref)

    def put(block, there, value):
        near_ref[jnp.where(there, rank_of(block, here_ref, outer_count, inner_count), spare)] = value

    take_in(put, here_ref, -1, outer_refs, inner_ref)
    own_acc_ref[...] = jnp.zeros_like(own_acc_ref)
    all_acc_ref[...] = jnp.zeros_like(all_acc_ref)
    forward_ref[...] = jnp.zeros_like(forward_ref)
    backward_ref[...] = jnp.zeros_like(backward_ref)

    def own_columns(ref):
        return [ref.at[:, c * LANES : (c + 1) * LANES] for c in range(chunks)]

    compact(starts_ref, [(target_pairs_ref, target_ref), (source_pairs_ref, source_ref)])
    position = source_ref[...]
    absent = REACH - upper_blocks(here_ref[1], inner_count)
    after_self = position >= cells + (here_ref[0] + 1) * LANES
    after_upper = position >= cells + (outer_count + REACH) * LANES
    source_ref[...] = position - jnp.where(after_self, LANES, 0) - jnp.where(after_upper, absent * LANES, 0)
    fetches[3].wait()
    turn_matrices(native_ref, t_ref)
    steps = (starts_ref[starts_ref.shape[0] - 1] + (WIDTH - 1)) // WIDTH
    low_lanes = lax.broadcasted_iota(jnp.int32, (terms, 2 * LANES), 1) & (LANES - 1)

    once = lax.broadcasted_iota(jnp.int32, (grains * terms, LANES), 1) < terms

    def scatter(group):
        first = jnp.maximum(group, 0) * per_step
        own_acc_ref[...] += scatter_product(index_row(target_ref, first, per_step), own_half, forward_ref[...])
        all_acc_ref[...] += scatter_product(index_row(source_ref, first, per_step), all_half, backward_ref[...])

    def step(group, carry):
        scatter(group - 1)
        ahead, back = [], []
        targets = fold_columns(fold_ref, parts, index_row(target_ref, group * per_step, per_step))
        for q in range(per_step):
            row = group * per_step + q
            sources = gather_columns(
                own_columns(x_ref) + [near_ref.at[k] for k in range(spare)], source_ref[pl.ds(row, 1), :]
            )
            columns = jnp.concatenate([stack_parts(sources), targets[:, q * LANES : (q + 1) * LANES]], axis=1)
            gap = jnp.zeros((LANES - parts, 2 * LANES), jnp.bfloat16)
            columns = jnp.concatenate([columns, gap, columns[:SHORT]], axis=0)
            high, low = [], []
            for g in range(grains):
                offset = offsets_ref[row * grains + g]
                matrix = t_ref[pl.ds(pl.multiple_of(offset * terms, 8), terms), :]
                high.append(matrix.astype(jnp.bfloat16).astype(jnp.float32))
                low.append(matrix - high[-1])
            high = jnp.concatenate(high, axis=0).astype(jnp.bfloat16)
            low = jnp.where(once, jnp.concatenate(low, axis=0), 0.0).astype(jnp.bfloat16)
            matrices = jnp.concatenate([high, low], axis=1)[:, : LANES + SHORT]
            moved = jnp.dot(matrices, columns, preferred_element_type=jnp.float32)
            total = moved[:terms]
            for g in range(1, grains):
                total = jnp.where(low_lanes >= g * GRAIN, moved[g * terms : (g + 1) * terms], total)
            total = stack_parts(total)
            ahead.append(total[:, :LANES])
            back.append(total[:, LANES:])
        for q in range(per_step):
            forward_ref[:, q * LANES : (q + 1) * LANES] = ahead[q]
            backward_ref[:, q * LANES : (q + 1) * LANES] = back[q]
        return carry

    lax.fori_loop(0, steps, step, 0)
    scatter(steps - 1)
    everywhere = unfold(all_acc_ref, terms) * sign_ref[...]
    own_ref[...] = unfold(own_acc_ref, terms) + everywhere[:, :cells]
    for k in range(spare):
        near_ref[k] = everywhere[:, cells + k * LANES : cells + (k + 1) * LANES]
    near_ref[spare] = jnp.zeros((terms, LANES), jnp.float32)

    def read(block, there):
        return near_ref[jnp.where(there, rank_of(block, here_ref, outer_count, inner_count), spare)]

    hand_out(read, here_ref, 1, outer_back_refs, inner_back_ref)


def translate(starts, offsets, here, pair_target, pair_source, trans, x, sign, inner, outer):
    terms, cells = x.shape
    offset_count = pair_target.shape[0]
    row_count = offsets.shape[0] * GRAIN // LANES
    hbm = pl.BlockSpec(memory_space=pltpu.HBM)
    outer_count = len(outer)
    near_count = most_blocks(outer_count + 1, inner.shape[0])
    own_half = cells // 2
    all_half = -(-(cells + near_count * LANES) // (2 * LANES)) * LANES
    smem = pl.BlockSpec(memory_space=pltpu.SMEM)
    vmem = pl.BlockSpec(memory_space=pltpu.VMEM)
    own, inner_back, *outer_back = pl.pallas_call(
        translate_kernel,
        out_shape=[jax.ShapeDtypeStruct(like.shape, jnp.float32) for like in (x, inner, *outer)],
        in_specs=[smem] * 3 + [hbm] * 4 + [vmem] * (2 + outer_count),
        out_specs=[vmem] * (2 + outer_count),
        scratch_shapes=[
            pltpu.VMEM(pair_target.shape, jnp.int32),
            pltpu.VMEM(pair_source.shape, jnp.int32),
            pltpu.VMEM((terms, terms, offset_count), jnp.float32),
            pltpu.VMEM((terms, cells), jnp.float32),
            pltpu.VMEM((row_count, LANES), jnp.int32),
            pltpu.VMEM((row_count, LANES), jnp.int32),
            pltpu.VMEM((offset_count * terms, LANES), jnp.float32),
            pltpu.VMEM((2 * terms * (cells // FOLD), FOLD), jnp.bfloat16),
            pltpu.VMEM((near_count + 1, terms, LANES), jnp.float32),
            pltpu.VMEM((2 * terms, WIDTH), jnp.bfloat16),
            pltpu.VMEM((2 * terms, WIDTH), jnp.bfloat16),
            pltpu.VMEM((own_half, 2 * LANES), jnp.float32),
            pltpu.VMEM((all_half, 2 * LANES), jnp.float32),
            pltpu.SemaphoreType.DMA((4,)),
        ],
        compiler_params=pltpu.CompilerParams(vmem_limit_bytes=VMEM_LIMIT),
        cost_estimate=pl.CostEstimate(flops=100_000_000_000, bytes_accessed=12_000_000, transcendentals=0),
    )(starts, offsets, here, pair_target, pair_source, trans.transpose(1, 2, 0), x, sign, inner, *outer)
    return own, inner_back, outer_back


def pack_kernel(here_ref, send_ref, multipoles_ref, inner_ref, *refs):
    outer_refs, (index_ref, x_ref, ready) = refs[:-3], refs[-3:]
    cells = x_ref.shape[1]
    fetches = [
        pltpu.make_async_copy(send_ref, index_ref, ready.at[0]),
        pltpu.make_async_copy(multipoles_ref, x_ref, ready.at[1]),
    ]
    for fetch in fetches:
        fetch.start()
    for fetch in fetches:
        fetch.wait()

    def read(block, there):
        index = index_ref[:, pl.ds(pl.multiple_of(block * LANES, LANES), LANES)]
        index = index if there is True else jnp.where(there, index, -1)
        return gather_columns([x_ref.at[:, c * LANES : (c + 1) * LANES] for c in range(cells // LANES)], index)

    hand_out(read, here_ref, -1, outer_refs, inner_ref)


def pack(here, index, x, outer_count, inner_count):
    smem = pl.BlockSpec(memory_space=pltpu.SMEM)
    vmem = pl.BlockSpec(memory_space=pltpu.VMEM)
    hbm = pl.BlockSpec(memory_space=pltpu.HBM)
    block = (x.shape[0], LANES)
    inner, *outer = pl.pallas_call(
        pack_kernel,
        out_shape=[jax.ShapeDtypeStruct((inner_count, *block), jnp.float32)]
        + [jax.ShapeDtypeStruct(block, jnp.float32)] * (outer_count - 1),
        in_specs=[smem, hbm, hbm],
        out_specs=[vmem] * outer_count,
        scratch_shapes=[
            pltpu.VMEM(index.shape, jnp.int32),
            pltpu.VMEM(x.shape, jnp.float32),
            pltpu.SemaphoreType.DMA((2,)),
        ],
        compiler_params=pltpu.CompilerParams(vmem_limit_bytes=PACK_LIMIT),
    )(here, index, x)
    return inner, outer


def collect_kernel(here_ref, index_ref, base_ref, inner_ref, *refs):
    outer_refs, (out_ref, near_ref, acc_ref) = refs[:-3], refs[-3:]
    terms, cells = base_ref.shape
    half = cells // 2
    near_ref[here_ref[0]] = jnp.zeros((terms, LANES), jnp.float32)

    def put(block, there, value):
        near_ref[block] = jnp.where(there, value, 0.0)

    take_in(put, here_ref, 1, outer_refs, inner_ref)
    parts = stack_parts(jnp.concatenate([near_ref[k] for k in range(near_ref.shape[0])], axis=1))
    acc_ref[...] = scatter_product(index_ref[...], half, parts)
    out_ref[...] = base_ref[...] + unfold(acc_ref, terms)


def collect(here, index, base, inner, outer):
    terms, cells = base.shape
    smem = pl.BlockSpec(memory_space=pltpu.SMEM)
    vmem = pl.BlockSpec(memory_space=pltpu.VMEM)
    return pl.pallas_call(
        collect_kernel,
        out_shape=jax.ShapeDtypeStruct(base.shape, jnp.float32),
        in_specs=[smem] + [vmem] * (3 + len(outer)),
        out_specs=vmem,
        scratch_shapes=[
            pltpu.VMEM((len(outer) + 1 + 2 * REACH, terms, LANES), jnp.float32),
            pltpu.VMEM((cells // 2, 2 * LANES), jnp.float32),
        ],
        compiler_params=pltpu.CompilerParams(vmem_limit_bytes=SMALL_LIMIT),
    )(here, index, base, inner, *outer)


def exchange(inner, outer):
    count = len(outer) + 1
    outer = [
        lax.ppermute(block, "gx", [(p, (p + k + 1) % count) for p in range(count)]) for k, block in enumerate(outer)
    ]
    return lax.all_to_all(inner, "gy", split_axis=0, concat_axis=0, tiled=True), outer


def per_device(multipoles, trans, pair_target, pair_source, send_list):
    offset_count, term_count, _ = trans.shape
    outer_count = lax.axis_size("gx")
    inner_count = lax.axis_size("gy")
    here = jnp.stack([lax.axis_index("gx"), lax.axis_index("gy")]).astype(jnp.int32)
    inner, outer = exchange(*pack(here, send_list, multipoles, outer_count, inner_count))

    used = jnp.sum((pair_target >= 0).astype(jnp.int32), axis=1)
    grains = (used + (GRAIN - 1)) // GRAIN
    ends = jnp.cumsum(grains)
    starts = jnp.concatenate([jnp.zeros((1,), jnp.int32), ends]) * GRAIN
    grain_count = -(-pair_target.size // WIDTH) * (WIDTH // GRAIN) + 2 * WIDTH // GRAIN
    grain_index = jnp.arange(grain_count, dtype=jnp.int32)
    offsets = jnp.sum((ends[None, :] <= grain_index[:, None]).astype(jnp.int32), axis=1)
    offsets = jnp.minimum(offsets, offset_count - 1)

    sign = parity_signs(term_count)[:, None]
    own, inner_back, outer_back = translate(
        starts, offsets, here, pair_target, pair_source, trans, multipoles, sign, inner, outer
    )
    return collect(here, send_list, own, *exchange(inner_back, outer_back))


def solution(mesh):
    placed = (
        P(None, ("gx", "gy")),
        P(),
        P(None, ("gx", "gy")),
        P(None, ("gx", "gy")),
        P(("gx", "gy"), None),
    )
    return jax.shard_map(
        per_device, mesh=mesh, in_specs=placed, out_specs=P(None, ("gx", "gy")), check_vma=False
    )
```

```python
import functools

import jax
import jax.numpy as jnp
from jax import lax
from jax.experimental import pallas as pl
from jax.experimental.pallas import tpu as pltpu
from jax.sharding import PartitionSpec as P

REACH = 4
LANES = 128
SUBLANES = 16
WIDTH = 1024
GRAIN = 32
FOLD = 256
SCRATCHES = 14
SHORT = 64
PACK_LIMIT = 60 * 1024 * 1024
VMEM_LIMIT = 53 * 1024 * 1024
SMALL_LIMIT = 16 * 1024 * 1024


def parity_signs(term_count):
    term_index = jnp.arange(term_count, dtype=jnp.int32)
    degree = (term_index >= 1).astype(jnp.int32) + (term_index >= 4).astype(jnp.int32)
    degree = degree + (term_index >= 10).astype(jnp.int32) + (term_index >= 20).astype(jnp.int32)
    degree = degree + (term_index >= 35).astype(jnp.int32)
    return jnp.where(degree % 2 == 0, 1.0, -1.0).astype(jnp.float32)


def hot_columns(places, size):
    count = places[0].shape[1]
    tall = (SUBLANES, count)
    one, none = jnp.ones((), jnp.bfloat16), jnp.zeros((), jnp.bfloat16)
    row = lax.broadcasted_iota(jnp.int32, tall, 0).astype(jnp.float32)
    rows = [(row + float(k)).astype(jnp.bfloat16) for k in range(0, size, SUBLANES)]
    blocks = []
    for place in places:
        wanted = jnp.broadcast_to(place.astype(jnp.float32), tall).astype(jnp.bfloat16)
        blocks += [jnp.where(one_row == wanted, one, none) for one_row in rows]
    return jnp.concatenate(blocks, axis=0)


def stack_parts(values):
    high = values.astype(jnp.bfloat16).astype(jnp.float32)
    return jnp.concatenate([high, values - high], axis=0).astype(jnp.bfloat16)


def scatter_product(index_row, half, parts):
    rows, count = parts.shape
    upper = jnp.broadcast_to(index_row >= half, (rows, count))
    none = jnp.zeros((), jnp.bfloat16)
    pad = jnp.zeros((LANES - rows, count), jnp.bfloat16)
    spread = jnp.concatenate([jnp.where(upper, none, parts), pad, jnp.where(upper, parts, none), pad], axis=0)
    place = jnp.where(index_row >= half, index_row - half, index_row)
    hot = hot_columns([place - j * LANES for j in range(half // LANES)], LANES)
    return lax.dot_general(
        hot, spread, (((1,), (1,)), ((), ())), preferred_element_type=jnp.float32
    )


def unfold(acc_ref, terms):
    sides = []
    for side in range(2):
        turned = acc_ref[:, side * LANES : (side + 1) * LANES].T
        sides.append(turned[:terms] + turned[terms : 2 * terms])
    return jnp.concatenate(sides, axis=1)


def pick(options, which):
    chosen = options[0]
    for k in range(1, len(options)):
        chosen = jnp.where(which == k, options[k], chosen)
    return chosen


def batch_of(count, most):
    return max(k for k in range(1, most + 1) if count % k == 0)


def compact(starts_ref, tables):
    offset_count, slot_count = tables[0][0].shape
    pieces = slot_count // LANES
    for _, out_ref in tables:
        out_ref[...] = jnp.full(out_ref.shape, -1, jnp.int32)
    lane = lax.broadcasted_iota(jnp.int32, (8, LANES), 1)
    empty = jnp.full((8, LANES), -1, jnp.int32)
    batch = batch_of(offset_count, 4)

    def place(step, kept):
        kept = list(kept)
        for u in range(batch):
            offset = step * batch + u
            start = starts_ref[offset]
            row, shift = start >> 7, start & (LANES - 1)
            crossed = (starts_ref[offset + 1] >> 7) - row
            inside = lane >= shift
            for k, (pairs_ref, out_ref) in enumerate(tables):
                line = pairs_ref[pl.ds(offset, 1), :]
                turned = [
                    pltpu.roll(jnp.broadcast_to(line[:, q * LANES : (q + 1) * LANES], (8, LANES)), shift, 1)
                    for q in range(pieces)
                ]
                turned = [kept[k], *turned, empty]
                tiles = [jnp.where(inside, turned[q + 1], turned[q]) for q in range(pieces + 1)]
                for q, tile in enumerate(tiles):
                    out_ref[pl.ds(row + q, 1), :] = tile[:1]
                kept[k] = pick(tiles, crossed)
        return tuple(kept)

    lax.fori_loop(0, offset_count // batch, place, (empty,) * len(tables))


def turn_matrices(t_ref, matrix_ref):
    terms, _, offset_count = t_ref.shape
    turns = batch_of(terms, 4)

    def turn(step, carry):
        for u in range(turns):
            i = step * turns + u
            parts = stack_parts(t_ref[i]).T.astype(jnp.float32)
            pad = jnp.zeros((offset_count, LANES - 2 * terms), jnp.float32)
            matrix_ref[pl.ds(i, offset_count, stride=terms), :] = jnp.concatenate([parts, pad], axis=1)
        return carry

    lax.fori_loop(0, terms // turns, turn, 0)


def index_row(ref, first, count):
    return jnp.concatenate([ref[pl.ds(first + q, 1), :] for q in range(count)], axis=1)


def gather_columns(parts, index):
    terms = parts[0].shape[0]
    lane = jnp.broadcast_to(index & (LANES - 1), (terms, LANES))
    chunk = jnp.broadcast_to(index >> 7, (8, LANES))
    picked = [jnp.zeros((8, LANES), jnp.float32)] * (terms // 8)
    for c, part in enumerate(parts):
        found = jnp.take_along_axis(part[...], lane, axis=1, mode="promise_in_bounds")
        here = chunk == c
        picked = [jnp.where(here, found[8 * r : 8 * r + 8], some) for r, some in enumerate(picked)]
    return jnp.concatenate(picked, axis=0)


def fold_columns(fold_ref, parts, index):
    count = index.shape[1]
    hot = hot_columns([index & (FOLD - 1)], FOLD)
    found = jnp.dot(fold_ref[...], hot, preferred_element_type=jnp.float32)
    chunk = jnp.broadcast_to(index >> (FOLD.bit_length() - 1), (8, count))
    masks = [chunk == c for c in range(fold_ref.shape[0] // parts)]
    picked = []
    for r in range(0, parts, 8):
        some = jnp.zeros((8, count), jnp.float32)
        for c, mask in enumerate(masks):
            some = jnp.where(mask, found[c * parts + r : c * parts + r + 8], some)
        picked.append(some)
    return jnp.concatenate(picked, axis=0)


def block_for(place, here, sign):
    distance = (place - here) * sign
    block = jnp.where(distance > 0, distance - 1, REACH - 1 - distance)
    there = (distance != 0) & (distance <= REACH) & (distance >= -REACH)
    return jnp.where(there, block, 0), there


def sender_of(block, here, sign, count):
    step = block + 1 if block < REACH else REACH - 1 - block
    place = here - step * sign
    return jnp.clip(place, 0, count - 1), (place >= 0) & (place < count)


def turned(place, count):
    return jnp.where(place >= count, place - count, jnp.where(place < 0, place + count, place))


def upper_blocks(here, count):
    return jnp.minimum(count - 1 - here, REACH)


def rank_of(block, here_ref, outer_count, inner_count):
    outer = block - jnp.where(block > here_ref[0], 1, 0)
    lower = block - 1 - REACH + upper_blocks(here_ref[1], inner_count)
    return jnp.where(block < outer_count, outer, jnp.where(block < outer_count + REACH, block - 1, lower))


def most_blocks(outer_count, inner_count):
    along = [min(REACH, inner_count - 1 - p) + min(REACH, p) for p in range(inner_count)]
    return outer_count - 1 + max(along)


def hand_out(read, here_ref, sign, outer_refs, inner_ref):
    outer_count = len(outer_refs) + 1
    for k, ref in enumerate(outer_refs):
        ref[...] = read(turned(here_ref[0] + k + 1, outer_count), True)

    def hand(place, carry):
        block, there = block_for(place, here_ref[1], sign)
        inner_ref[place] = read(outer_count + block, there)
        return carry

    lax.fori_loop(0, inner_ref.shape[0], hand, 0, unroll=4)


def take_in(put, here_ref, sign, outer_refs, inner_ref):
    outer_count = len(outer_refs) + 1
    for k, ref in enumerate(outer_refs):
        put(turned(here_ref[0] - k - 1, outer_count), True, ref[...])
    for block in range(2 * REACH):
        sender, there = sender_of(block, here_ref[1], sign, inner_ref.shape[0])
        put(outer_count + block, there, inner_ref[sender])


def translate_kernel(*refs):
    outer_count = (len(refs) - SCRATCHES - 11) // 2
    inputs, refs = refs[:9], refs[9:]
    outer_refs, refs = refs[:outer_count], refs[outer_count:]
    own_ref, inner_back_ref, refs = refs[0], refs[1], refs[2:]
    outer_back_refs, refs = refs[:outer_count], refs[outer_count:]
    translate_body(*inputs, outer_refs, own_ref, inner_back_ref, outer_back_refs, *refs)


def translate_body(
    starts_ref, offsets_ref, here_ref, pair_target_ref, pair_source_ref, trans_ref, multipoles_ref, sign_ref, inner_ref,
    outer_refs, own_ref, inner_back_ref, outer_back_refs,
    target_pairs_ref, source_pairs_ref, native_ref, x_ref, target_ref, source_ref, t_ref,
    fold_ref, near_ref, forward_ref, backward_ref, own_acc_ref, all_acc_ref, ready
):
    fetches = [
        pltpu.make_async_copy(here, there, ready.at[k])
        for k, (here, there) in enumerate(
            [
                (pair_target_ref, target_pairs_ref),
                (pair_source_ref, source_pairs_ref),
                (multipoles_ref, x_ref),
                (trans_ref, native_ref),
            ]
        )
    ]
    for fetch in fetches:
        fetch.start()
    terms, cells = x_ref.shape
    outer_count, inner_count = len(outer_refs) + 1, inner_ref.shape[0]
    spare = near_ref.shape[0] - 1
    chunks = cells // LANES
    own_half = cells // 2
    all_half = all_acc_ref.shape[0]
    parts = 2 * terms
    per_step = WIDTH // LANES
    grains = LANES // GRAIN

    for fetch in fetches[:3]:
        fetch.wait()
    folds = cells // FOLD
    for c in range(folds):
        fold_ref[c * parts : (c + 1) * parts, :] = stack_parts(x_ref[:, c * FOLD : (c + 1) * FOLD] * sign_ref[...])
    near_ref[...] = jnp.zeros_like(near_ref)

    def put(block, there, value):
        near_ref[jnp.where(there, rank_of(block, here_ref, outer_count, inner_count), spare)] = value

    take_in(put, here_ref, -1, outer_refs, inner_ref)
    own_acc_ref[...] = jnp.zeros_like(own_acc_ref)
    all_acc_ref[...] = jnp.zeros_like(all_acc_ref)
    forward_ref[...] = jnp.zeros_like(forward_ref)
    backward_ref[...] = jnp.zeros_like(backward_ref)

    def own_columns(ref):
        return [ref.at[:, c * LANES : (c + 1) * LANES] for c in range(chunks)]

    compact(starts_ref, [(target_pairs_ref, target_ref), (source_pairs_ref, source_ref)])
    position = source_ref[...]
    absent = REACH - upper_blocks(here_ref[1], inner_count)
    after_self = position >= cells + (here_ref[0] + 1) * LANES
    after_upper = position >= cells + (outer_count + REACH) * LANES
    source_ref[...] = position - jnp.where(after_self, LANES, 0) - jnp.where(after_upper, absent * LANES, 0)
    fetches[3].wait()
    turn_matrices(native_ref, t_ref)
    steps = (starts_ref[starts_ref.shape[0] - 1] + (WIDTH - 1)) // WIDTH
    low_lanes = lax.broadcasted_iota(jnp.int32, (terms, 2 * LANES), 1) & (LANES - 1)

    def scatter(group):
        first = jnp.maximum(group, 0) * per_step
        own_acc_ref[...] += scatter_product(index_row(target_ref, first, per_step), own_half, forward_ref[...])
        all_acc_ref[...] += scatter_product(index_row(source_ref, first, per_step), all_half, backward_ref[...])

    def step(group, carry):
        scatter(group - 1)
        ahead, back = [], []
        targets = fold_columns(fold_ref, parts, index_row(target_ref, group * per_step, per_step))
        for q in range(per_step):
            row = group * per_step + q
            sources = gather_columns(
                own_columns(x_ref) + [near_ref.at[k] for k in range(spare)], source_ref[pl.ds(row, 1), :]
            )
            here = slice(q * LANES, (q + 1) * LANES)
            source_high = sources.astype(jnp.bfloat16).astype(jnp.float32)
            high = jnp.concatenate([source_high, targets[:terms, here]], axis=1)
            low = jnp.concatenate([sources - source_high, targets[terms:, here]], axis=1)
            gap = jnp.zeros((LANES - parts, 2 * LANES), jnp.float32)
            rest = jnp.zeros((SHORT - terms, 2 * LANES), jnp.float32)
            columns = jnp.concatenate([high, high, gap, low, rest], axis=0).astype(jnp.bfloat16)
            matrices = [
                t_ref[pl.ds(pl.multiple_of(offsets_ref[row * grains + g] * terms, 8), terms), :] for g in range(grains)
            ]
            matrices = jnp.concatenate(matrices, axis=0).astype(jnp.bfloat16)
            matrices = jnp.concatenate([matrices, matrices[:, :SHORT]], axis=1)
            moved = jnp.dot(matrices, columns, preferred_element_type=jnp.float32)
            total = moved[:terms]
            for g in range(1, grains):
                total = jnp.where(low_lanes >= g * GRAIN, moved[g * terms : (g + 1) * terms], total)
            total = stack_parts(total)
            ahead.append(total[:, :LANES])
            back.append(total[:, LANES:])
        for q in range(per_step):
            forward_ref[:, q * LANES : (q + 1) * LANES] = ahead[q]
            backward_ref[:, q * LANES : (q + 1) * LANES] = back[q]
        return carry

    lax.fori_loop(0, steps, step, 0)
    scatter(steps - 1)
    everywhere = unfold(all_acc_ref, terms) * sign_ref[...]
    own_ref[...] = unfold(own_acc_ref, terms) + everywhere[:, :cells]
    for k in range(spare):
        near_ref[k] = everywhere[:, cells + k * LANES : cells + (k + 1) * LANES]
    near_ref[spare] = jnp.zeros((terms, LANES), jnp.float32)

    def read(block, there):
        return near_ref[jnp.where(there, rank_of(block, here_ref, outer_count, inner_count), spare)]

    hand_out(read, here_ref, 1, outer_back_refs, inner_back_ref)


def translate(starts, offsets, here, pair_target, pair_source, trans, x, sign, inner, outer):
    terms, cells = x.shape
    offset_count = pair_target.shape[0]
    row_count = offsets.shape[0] * GRAIN // LANES
    hbm = pl.BlockSpec(memory_space=pltpu.HBM)
    outer_count = len(outer)
    near_count = most_blocks(outer_count + 1, inner.shape[0])
    own_half = cells // 2
    all_half = -(-(cells + near_count * LANES) // (2 * LANES)) * LANES
    smem = pl.BlockSpec(memory_space=pltpu.SMEM)
    vmem = pl.BlockSpec(memory_space=pltpu.VMEM)
    own, inner_back, *outer_back = pl.pallas_call(
        translate_kernel,
        out_shape=[jax.ShapeDtypeStruct(like.shape, jnp.float32) for like in (x, inner, *outer)],
        in_specs=[smem] * 3 + [hbm] * 4 + [vmem] * (2 + outer_count),
        out_specs=[vmem] * (2 + outer_count),
        scratch_shapes=[
            pltpu.VMEM(pair_target.shape, jnp.int32),
            pltpu.VMEM(pair_source.shape, jnp.int32),
            pltpu.VMEM((terms, terms, offset_count), jnp.float32),
            pltpu.VMEM((terms, cells), jnp.float32),
            pltpu.VMEM((row_count, LANES), jnp.int32),
            pltpu.VMEM((row_count, LANES), jnp.int32),
            pltpu.VMEM((offset_count * terms, LANES), jnp.float32),
            pltpu.VMEM((2 * terms * (cells // FOLD), FOLD), jnp.bfloat16),
            pltpu.VMEM((near_count + 1, terms, LANES), jnp.float32),
            pltpu.VMEM((2 * terms, WIDTH), jnp.bfloat16),
            pltpu.VMEM((2 * terms, WIDTH), jnp.bfloat16),
            pltpu.VMEM((own_half, 2 * LANES), jnp.float32),
            pltpu.VMEM((all_half, 2 * LANES), jnp.float32),
            pltpu.SemaphoreType.DMA((4,)),
        ],
        compiler_params=pltpu.CompilerParams(vmem_limit_bytes=VMEM_LIMIT),
        cost_estimate=pl.CostEstimate(flops=100_000_000_000, bytes_accessed=12_000_000, transcendentals=0),
    )(starts, offsets, here, pair_target, pair_source, trans.transpose(1, 2, 0), x, sign, inner, *outer)
    return own, inner_back, outer_back


def pack_kernel(here_ref, send_ref, multipoles_ref, inner_ref, *refs):
    outer_refs, (index_ref, x_ref, ready) = refs[:-3], refs[-3:]
    cells = x_ref.shape[1]
    fetches = [
        pltpu.make_async_copy(send_ref, index_ref, ready.at[0]),
        pltpu.make_async_copy(multipoles_ref, x_ref, ready.at[1]),
    ]
    for fetch in fetches:
        fetch.start()
    for fetch in fetches:
        fetch.wait()

    def read(block, there):
        index = index_ref[:, pl.ds(pl.multiple_of(block * LANES, LANES), LANES)]
        index = index if there is True else jnp.where(there, index, -1)
        return gather_columns([x_ref.at[:, c * LANES : (c + 1) * LANES] for c in range(cells // LANES)], index)

    hand_out(read, here_ref, -1, outer_refs, inner_ref)


def pack(here, index, x, outer_count, inner_count):
    smem = pl.BlockSpec(memory_space=pltpu.SMEM)
    vmem = pl.BlockSpec(memory_space=pltpu.VMEM)
    hbm = pl.BlockSpec(memory_space=pltpu.HBM)
    block = (x.shape[0], LANES)
    inner, *outer = pl.pallas_call(
        pack_kernel,
        out_shape=[jax.ShapeDtypeStruct((inner_count, *block), jnp.float32)]
        + [jax.ShapeDtypeStruct(block, jnp.float32)] * (outer_count - 1),
        in_specs=[smem, hbm, hbm],
        out_specs=[vmem] * outer_count,
        scratch_shapes=[
            pltpu.VMEM(index.shape, jnp.int32),
            pltpu.VMEM(x.shape, jnp.float32),
            pltpu.SemaphoreType.DMA((2,)),
        ],
        compiler_params=pltpu.CompilerParams(vmem_limit_bytes=PACK_LIMIT),
    )(here, index, x)
    return inner, outer


def collect_kernel(here_ref, index_ref, base_ref, inner_ref, *refs):
    outer_refs, (out_ref, near_ref, acc_ref) = refs[:-3], refs[-3:]
    terms, cells = base_ref.shape
    half = cells // 2
    near_ref[here_ref[0]] = jnp.zeros((terms, LANES), jnp.float32)

    def put(block, there, value):
        near_ref[block] = jnp.where(there, value, 0.0)

    take_in(put, here_ref, 1, outer_refs, inner_ref)
    parts = stack_parts(jnp.concatenate([near_ref[k] for k in range(near_ref.shape[0])], axis=1))
    acc_ref[...] = scatter_product(index_ref[...], half, parts)
    out_ref[...] = base_ref[...] + unfold(acc_ref, terms)


def collect(here, index, base, inner, outer):
    terms, cells = base.shape
    smem = pl.BlockSpec(memory_space=pltpu.SMEM)
    vmem = pl.BlockSpec(memory_space=pltpu.VMEM)
    return pl.pallas_call(
        collect_kernel,
        out_shape=jax.ShapeDtypeStruct(base.shape, jnp.float32),
        in_specs=[smem] + [vmem] * (3 + len(outer)),
        out_specs=vmem,
        scratch_shapes=[
            pltpu.VMEM((len(outer) + 1 + 2 * REACH, terms, LANES), jnp.float32),
            pltpu.VMEM((cells // 2, 2 * LANES), jnp.float32),
        ],
        compiler_params=pltpu.CompilerParams(vmem_limit_bytes=SMALL_LIMIT),
    )(here, index, base, inner, *outer)


def exchange(inner, outer):
    count = len(outer) + 1
    outer = [
        lax.ppermute(block, "gx", [(p, (p + k + 1) % count) for p in range(count)]) for k, block in enumerate(outer)
    ]
    return lax.all_to_all(inner, "gy", split_axis=0, concat_axis=0, tiled=True), outer


def per_device(multipoles, trans, pair_target, pair_source, send_list):
    offset_count, term_count, _ = trans.shape
    outer_count = lax.axis_size("gx")
    inner_count = lax.axis_size("gy")
    here = jnp.stack([lax.axis_index("gx"), lax.axis_index("gy")]).astype(jnp.int32)
    inner, outer = exchange(*pack(here, send_list, multipoles, outer_count, inner_count))

    used = jnp.sum((pair_target >= 0).astype(jnp.int32), axis=1)
    grains = (used + (GRAIN - 1)) // GRAIN
    ends = jnp.cumsum(grains)
    starts = jnp.concatenate([jnp.zeros((1,), jnp.int32), ends]) * GRAIN
    grain_count = -(-pair_target.size // WIDTH) * (WIDTH // GRAIN) + 2 * WIDTH // GRAIN
    grain_index = jnp.arange(grain_count, dtype=jnp.int32)
    offsets = jnp.sum((ends[None, :] <= grain_index[:, None]).astype(jnp.int32), axis=1)
    offsets = jnp.minimum(offsets, offset_count - 1)

    sign = parity_signs(term_count)[:, None]
    own, inner_back, outer_back = translate(
        starts, offsets, here, pair_target, pair_source, trans, multipoles, sign, inner, outer
    )
    return collect(here, send_list, own, *exchange(inner_back, outer_back))


def solution(mesh):
    placed = (
        P(None, ("gx", "gy")),
        P(),
        P(None, ("gx", "gy")),
        P(None, ("gx", "gy")),
        P(("gx", "gy"), None),
    )
    return jax.shard_map(
        per_device, mesh=mesh, in_specs=placed, out_specs=P(None, ("gx", "gy")), check_vma=False
    )
```

```python
import functools

import jax
import jax.numpy as jnp
from jax import lax
from jax.experimental import pallas as pl
from jax.experimental.pallas import tpu as pltpu
from jax.sharding import PartitionSpec as P

REACH = 4
LANES = 128
SUBLANES = 16
WIDTH = 1024
GRAIN = 64
TOGETHER = 2
FOLD = 256
SCRATCHES = 14
SHORT = 64
PACK_LIMIT = 60 * 1024 * 1024
VMEM_LIMIT = 53 * 1024 * 1024
SMALL_LIMIT = 16 * 1024 * 1024


def parity_signs(term_count):
    term_index = jnp.arange(term_count, dtype=jnp.int32)
    degree = (term_index >= 1).astype(jnp.int32) + (term_index >= 4).astype(jnp.int32)
    degree = degree + (term_index >= 10).astype(jnp.int32) + (term_index >= 20).astype(jnp.int32)
    degree = degree + (term_index >= 35).astype(jnp.int32)
    return jnp.where(degree % 2 == 0, 1.0, -1.0).astype(jnp.float32)


def hot_columns(places, size):
    count = places[0].shape[1]
    tall = (SUBLANES, count)
    one, none = jnp.ones((), jnp.bfloat16), jnp.zeros((), jnp.bfloat16)
    row = lax.broadcasted_iota(jnp.int32, tall, 0).astype(jnp.float32)
    rows = [(row + float(k)).astype(jnp.bfloat16) for k in range(0, size, SUBLANES)]
    blocks = []
    for place in places:
        wanted = jnp.broadcast_to(place.astype(jnp.float32), tall).astype(jnp.bfloat16)
        blocks += [jnp.where(one_row == wanted, one, none) for one_row in rows]
    return jnp.concatenate(blocks, axis=0)


def stack_parts(values):
    high = values.astype(jnp.bfloat16).astype(jnp.float32)
    return jnp.concatenate([high, values - high], axis=0).astype(jnp.bfloat16)


def scatter_product(index_row, half, parts):
    rows, count = parts.shape
    upper = jnp.broadcast_to(index_row >= half, (rows, count))
    none = jnp.zeros((), jnp.bfloat16)
    pad = jnp.zeros((LANES - rows, count), jnp.bfloat16)
    spread = jnp.concatenate([jnp.where(upper, none, parts), pad, jnp.where(upper, parts, none), pad], axis=0)
    place = jnp.where(index_row >= half, index_row - half, index_row)
    hot = hot_columns([place - j * LANES for j in range(half // LANES)], LANES)
    return lax.dot_general(
        hot, spread, (((1,), (1,)), ((), ())), preferred_element_type=jnp.float32
    )


def unfold(acc_ref, terms):
    sides = []
    for side in range(2):
        turned = acc_ref[:, side * LANES : (side + 1) * LANES].T
        sides.append(turned[:terms] + turned[terms : 2 * terms])
    return jnp.concatenate(sides, axis=1)


def pick(options, which):
    chosen = options[0]
    for k in range(1, len(options)):
        chosen = jnp.where(which == k, options[k], chosen)
    return chosen


def batch_of(count, most):
    return max(k for k in range(1, most + 1) if count % k == 0)


def compact(starts_ref, tables):
    offset_count, slot_count = tables[0][0].shape
    pieces = slot_count // LANES
    for _, out_ref in tables:
        out_ref[...] = jnp.full(out_ref.shape, -1, jnp.int32)
    lane = lax.broadcasted_iota(jnp.int32, (8, LANES), 1)
    empty = jnp.full((8, LANES), -1, jnp.int32)
    batch = batch_of(offset_count, 4)

    def place(step, kept):
        kept = list(kept)
        for u in range(batch):
            offset = step * batch + u
            start = starts_ref[offset]
            row, shift = start >> 7, start & (LANES - 1)
            crossed = (starts_ref[offset + 1] >> 7) - row
            inside = lane >= shift
            for k, (pairs_ref, out_ref) in enumerate(tables):
                line = pairs_ref[pl.ds(offset, 1), :]
                turned = [
                    pltpu.roll(jnp.broadcast_to(line[:, q * LANES : (q + 1) * LANES], (8, LANES)), shift, 1)
                    for q in range(pieces)
                ]
                turned = [kept[k], *turned, empty]
                tiles = [jnp.where(inside, turned[q + 1], turned[q]) for q in range(pieces + 1)]
                for q, tile in enumerate(tiles):
                    out_ref[pl.ds(row + q, 1), :] = tile[:1]
                kept[k] = pick(tiles, crossed)
        return tuple(kept)

    lax.fori_loop(0, offset_count // batch, place, (empty,) * len(tables))


def turn_matrices(t_ref, matrix_ref):
    terms, _, offset_count = t_ref.shape
    turns = batch_of(terms, 4)

    def turn(step, carry):
        for u in range(turns):
            i = step * turns + u
            parts = stack_parts(t_ref[i]).T.astype(jnp.float32)
            pad = jnp.zeros((offset_count, LANES - 2 * terms), jnp.float32)
            matrix_ref[pl.ds(i, offset_count, stride=terms), :] = jnp.concatenate([parts, pad], axis=1)
        return carry

    lax.fori_loop(0, terms // turns, turn, 0)


def index_row(ref, first, count):
    return jnp.concatenate([ref[pl.ds(first + q, 1), :] for q in range(count)], axis=1)


def gather_columns(parts, rows):
    terms = parts[0].shape[0]
    lanes = [jnp.broadcast_to(index & (LANES - 1), (terms, LANES)) for index in rows]
    chunks = [jnp.broadcast_to(index >> 7, (8, LANES)) for index in rows]
    picked = [[jnp.zeros((8, LANES), jnp.float32)] * (terms // 8) for _ in rows]
    for c, part in enumerate(parts):
        cells = part[...]
        for k, lane in enumerate(lanes):
            found = jnp.take_along_axis(cells, lane, axis=1, mode="promise_in_bounds")
            here = chunks[k] == c
            picked[k] = [jnp.where(here, found[8 * r : 8 * r + 8], some) for r, some in enumerate(picked[k])]
    return [jnp.concatenate(some, axis=0) for some in picked]


def fold_columns(fold_ref, parts, index):
    count = index.shape[1]
    hot = hot_columns([index & (FOLD - 1)], FOLD)
    found = jnp.dot(fold_ref[...], hot, preferred_element_type=jnp.float32)
    chunk = jnp.broadcast_to(index >> (FOLD.bit_length() - 1), (8, count))
    masks = [chunk == c for c in range(fold_ref.shape[0] // parts)]
    picked = []
    for r in range(0, parts, 8):
        some = jnp.zeros((8, count), jnp.float32)
        for c, mask in enumerate(masks):
            some = jnp.where(mask, found[c * parts + r : c * parts + r + 8], some)
        picked.append(some)
    return jnp.concatenate(picked, axis=0)


def block_for(place, here, sign):
    distance = (place - here) * sign
    block = jnp.where(distance > 0, distance - 1, REACH - 1 - distance)
    there = (distance != 0) & (distance <= REACH) & (distance >= -REACH)
    return jnp.where(there, block, 0), there


def sender_of(block, here, sign, count):
    step = block + 1 if block < REACH else REACH - 1 - block
    place = here - step * sign
    return jnp.clip(place, 0, count - 1), (place >= 0) & (place < count)


def turned(place, count):
    return jnp.where(place >= count, place - count, jnp.where(place < 0, place + count, place))


def upper_blocks(here, count):
    return jnp.minimum(count - 1 - here, REACH)


def rank_of(block, here_ref, outer_count, inner_count):
    outer = block - jnp.where(block > here_ref[0], 1, 0)
    lower = block - 1 - REACH + upper_blocks(here_ref[1], inner_count)
    return jnp.where(block < outer_count, outer, jnp.where(block < outer_count + REACH, block - 1, lower))


def most_blocks(outer_count, inner_count):
    along = [min(REACH, inner_count - 1 - p) + min(REACH, p) for p in range(inner_count)]
    return outer_count - 1 + max(along)


def hand_out(read, here_ref, sign, outer_refs, inner_ref):
    outer_count = len(outer_refs) + 1
    for k, ref in enumerate(outer_refs):
        ref[...] = read(turned(here_ref[0] + k + 1, outer_count), True)

    def hand(place, carry):
        block, there = block_for(place, here_ref[1], sign)
        inner_ref[place] = read(outer_count + block, there)
        return carry

    lax.fori_loop(0, inner_ref.shape[0], hand, 0, unroll=4)


def take_in(put, here_ref, sign, outer_refs, inner_ref):
    outer_count = len(outer_refs) + 1
    for k, ref in enumerate(outer_refs):
        put(turned(here_ref[0] - k - 1, outer_count), True, ref[...])
    for block in range(2 * REACH):
        sender, there = sender_of(block, here_ref[1], sign, inner_ref.shape[0])
        put(outer_count + block, there, inner_ref[sender])


def translate_kernel(*refs):
    outer_count = (len(refs) - SCRATCHES - 11) // 2
    inputs, refs = refs[:9], refs[9:]
    outer_refs, refs = refs[:outer_count], refs[outer_count:]
    own_ref, inner_back_ref, refs = refs[0], refs[1], refs[2:]
    outer_back_refs, refs = refs[:outer_count], refs[outer_count:]
    translate_body(*inputs, outer_refs, own_ref, inner_back_ref, outer_back_refs, *refs)


def translate_body(
    starts_ref, offsets_ref, here_ref, pair_target_ref, pair_source_ref, trans_ref, multipoles_ref, sign_ref, inner_ref,
    outer_refs, own_ref, inner_back_ref, outer_back_refs,
    target_pairs_ref, source_pairs_ref, native_ref, x_ref, target_ref, source_ref, t_ref,
    fold_ref, near_ref, forward_ref, backward_ref, own_acc_ref, all_acc_ref, ready
):
    fetches = [
        pltpu.make_async_copy(here, there, ready.at[k])
        for k, (here, there) in enumerate(
            [
                (pair_target_ref, target_pairs_ref),
                (pair_source_ref, source_pairs_ref),
                (multipoles_ref, x_ref),
                (trans_ref, native_ref),
            ]
        )
    ]
    for fetch in fetches:
        fetch.start()
    terms, cells = x_ref.shape
    outer_count, inner_count = len(outer_refs) + 1, inner_ref.shape[0]
    spare = near_ref.shape[0] - 1
    chunks = cells // LANES
    own_half = cells // 2
    all_half = all_acc_ref.shape[0]
    parts = 2 * terms
    per_step = WIDTH // LANES
    grains = LANES // GRAIN

    for fetch in fetches[:3]:
        fetch.wait()
    folds = cells // FOLD
    for c in range(folds):
        fold_ref[c * parts : (c + 1) * parts, :] = stack_parts(x_ref[:, c * FOLD : (c + 1) * FOLD] * sign_ref[...])
    near_ref[...] = jnp.zeros_like(near_ref)

    def put(block, there, value):
        near_ref[jnp.where(there, rank_of(block, here_ref, outer_count, inner_count), spare)] = value

    take_in(put, here_ref, -1, outer_refs, inner_ref)
    own_acc_ref[...] = jnp.zeros_like(own_acc_ref)
    all_acc_ref[...] = jnp.zeros_like(all_acc_ref)
    forward_ref[...] = jnp.zeros_like(forward_ref)
    backward_ref[...] = jnp.zeros_like(backward_ref)

    def own_columns(ref):
        return [ref.at[:, c * LANES : (c + 1) * LANES] for c in range(chunks)]

    compact(starts_ref, [(target_pairs_ref, target_ref), (source_pairs_ref, source_ref)])
    position = source_ref[...]
    absent = REACH - upper_blocks(here_ref[1], inner_count)
    after_self = position >= cells + (here_ref[0] + 1) * LANES
    after_upper = position >= cells + (outer_count + REACH) * LANES
    source_ref[...] = position - jnp.where(after_self, LANES, 0) - jnp.where(after_upper, absent * LANES, 0)
    fetches[3].wait()
    turn_matrices(native_ref, t_ref)
    steps = (starts_ref[starts_ref.shape[0] - 1] + (WIDTH - 1)) // WIDTH
    low_lanes = lax.broadcasted_iota(jnp.int32, (terms, 2 * LANES), 1) & (LANES - 1)

    def scatter(group):
        first = jnp.maximum(group, 0) * per_step
        own_acc_ref[...] += scatter_product(index_row(target_ref, first, per_step), own_half, forward_ref[...])
        all_acc_ref[...] += scatter_product(index_row(source_ref, first, per_step), all_half, backward_ref[...])

    def step(group, carry):
        scatter(group - 1)
        ahead, back = [], []
        targets = fold_columns(fold_ref, parts, index_row(target_ref, group * per_step, per_step))
        for q in range(per_step):
            row = group * per_step + q
            if q % TOGETHER == 0:
                gathered = gather_columns(
                    own_columns(x_ref) + [near_ref.at[k] for k in range(spare)],
                    [source_ref[pl.ds(row + k, 1), :] for k in range(TOGETHER)],
                )
            sources = gathered[q % TOGETHER]
            here = slice(q * LANES, (q + 1) * LANES)
            source_high = sources.astype(jnp.bfloat16).astype(jnp.float32)
            high = jnp.concatenate([source_high, targets[:terms, here]], axis=1)
            low = jnp.concatenate([sources - source_high, targets[terms:, here]], axis=1)
            gap = jnp.zeros((LANES - parts, 2 * LANES), jnp.float32)
            rest = jnp.zeros((SHORT - terms, 2 * LANES), jnp.float32)
            columns = jnp.concatenate([high, high, gap, low, rest], axis=0).astype(jnp.bfloat16)
            matrices = [
                t_ref[pl.ds(pl.multiple_of(offsets_ref[row * grains + g] * terms, 8), terms), :] for g in range(grains)
            ]
            matrices = jnp.concatenate(matrices, axis=0).astype(jnp.bfloat16)
            matrices = jnp.concatenate([matrices, matrices[:, :SHORT]], axis=1)
            moved = jnp.dot(matrices, columns, preferred_element_type=jnp.float32)
            total = moved[:terms]
            for g in range(1, grains):
                total = jnp.where(low_lanes >= g * GRAIN, moved[g * terms : (g + 1) * terms], total)
            total = stack_parts(total)
            ahead.append(total[:, :LANES])
            back.append(total[:, LANES:])
        for q in range(per_step):
            forward_ref[:, q * LANES : (q + 1) * LANES] = ahead[q]
            backward_ref[:, q * LANES : (q + 1) * LANES] = back[q]
        return carry

    lax.fori_loop(0, steps, step, 0)
    scatter(steps - 1)
    everywhere = unfold(all_acc_ref, terms) * sign_ref[...]
    own_ref[...] = unfold(own_acc_ref, terms) + everywhere[:, :cells]
    for k in range(spare):
        near_ref[k] = everywhere[:, cells + k * LANES : cells + (k + 1) * LANES]
    near_ref[spare] = jnp.zeros((terms, LANES), jnp.float32)

    def read(block, there):
        return near_ref[jnp.where(there, rank_of(block, here_ref, outer_count, inner_count), spare)]

    hand_out(read, here_ref, 1, outer_back_refs, inner_back_ref)


def translate(starts, offsets, here, pair_target, pair_source, trans, x, sign, inner, outer):
    terms, cells = x.shape
    offset_count = pair_target.shape[0]
    row_count = offsets.shape[0] * GRAIN // LANES
    hbm = pl.BlockSpec(memory_space=pltpu.HBM)
    outer_count = len(outer)
    near_count = most_blocks(outer_count + 1, inner.shape[0])
    own_half = cells // 2
    all_half = -(-(cells + near_count * LANES) // (2 * LANES)) * LANES
    smem = pl.BlockSpec(memory_space=pltpu.SMEM)
    vmem = pl.BlockSpec(memory_space=pltpu.VMEM)
    own, inner_back, *outer_back = pl.pallas_call(
        translate_kernel,
        out_shape=[jax.ShapeDtypeStruct(like.shape, jnp.float32) for like in (x, inner, *outer)],
        in_specs=[smem] * 3 + [hbm] * 4 + [vmem] * (2 + outer_count),
        out_specs=[vmem] * (2 + outer_count),
        scratch_shapes=[
            pltpu.VMEM(pair_target.shape, jnp.int32),
            pltpu.VMEM(pair_source.shape, jnp.int32),
            pltpu.VMEM((terms, terms, offset_count), jnp.float32),
            pltpu.VMEM((terms, cells), jnp.float32),
            pltpu.VMEM((row_count, LANES), jnp.int32),
            pltpu.VMEM((row_count, LANES), jnp.int32),
            pltpu.VMEM((offset_count * terms, LANES), jnp.float32),
            pltpu.VMEM((2 * terms * (cells // FOLD), FOLD), jnp.bfloat16),
            pltpu.VMEM((near_count + 1, terms, LANES), jnp.float32),
            pltpu.VMEM((2 * terms, WIDTH), jnp.bfloat16),
            pltpu.VMEM((2 * terms, WIDTH), jnp.bfloat16),
            pltpu.VMEM((own_half, 2 * LANES), jnp.float32),
            pltpu.VMEM((all_half, 2 * LANES), jnp.float32),
            pltpu.SemaphoreType.DMA((4,)),
        ],
        compiler_params=pltpu.CompilerParams(vmem_limit_bytes=VMEM_LIMIT),
        cost_estimate=pl.CostEstimate(flops=100_000_000_000, bytes_accessed=12_000_000, transcendentals=0),
    )(starts, offsets, here, pair_target, pair_source, trans.transpose(1, 2, 0), x, sign, inner, *outer)
    return own, inner_back, outer_back


def pack_kernel(here_ref, send_ref, multipoles_ref, inner_ref, *refs):
    outer_refs, (index_ref, x_ref, ready) = refs[:-3], refs[-3:]
    cells = x_ref.shape[1]
    fetches = [
        pltpu.make_async_copy(send_ref, index_ref, ready.at[0]),
        pltpu.make_async_copy(multipoles_ref, x_ref, ready.at[1]),
    ]
    for fetch in fetches:
        fetch.start()
    for fetch in fetches:
        fetch.wait()

    def read(block, there):
        index = index_ref[:, pl.ds(pl.multiple_of(block * LANES, LANES), LANES)]
        index = index if there is True else jnp.where(there, index, -1)
        return gather_columns([x_ref.at[:, c * LANES : (c + 1) * LANES] for c in range(cells // LANES)], [index])[0]

    hand_out(read, here_ref, -1, outer_refs, inner_ref)


def pack(here, index, x, outer_count, inner_count):
    smem = pl.BlockSpec(memory_space=pltpu.SMEM)
    vmem = pl.BlockSpec(memory_space=pltpu.VMEM)
    hbm = pl.BlockSpec(memory_space=pltpu.HBM)
    block = (x.shape[0], LANES)
    inner, *outer = pl.pallas_call(
        pack_kernel,
        out_shape=[jax.ShapeDtypeStruct((inner_count, *block), jnp.float32)]
        + [jax.ShapeDtypeStruct(block, jnp.float32)] * (outer_count - 1),
        in_specs=[smem, hbm, hbm],
        out_specs=[vmem] * outer_count,
        scratch_shapes=[
            pltpu.VMEM(index.shape, jnp.int32),
            pltpu.VMEM(x.shape, jnp.float32),
            pltpu.SemaphoreType.DMA((2,)),
        ],
        compiler_params=pltpu.CompilerParams(vmem_limit_bytes=PACK_LIMIT),
    )(here, index, x)
    return inner, outer


def collect_kernel(here_ref, index_ref, base_ref, inner_ref, *refs):
    outer_refs, (out_ref, near_ref, acc_ref) = refs[:-3], refs[-3:]
    terms, cells = base_ref.shape
    half = cells // 2
    near_ref[here_ref[0]] = jnp.zeros((terms, LANES), jnp.float32)

    def put(block, there, value):
        near_ref[block] = jnp.where(there, value, 0.0)

    take_in(put, here_ref, 1, outer_refs, inner_ref)
    parts = stack_parts(jnp.concatenate([near_ref[k] for k in range(near_ref.shape[0])], axis=1))
    acc_ref[...] = scatter_product(index_ref[...], half, parts)
    out_ref[...] = base_ref[...] + unfold(acc_ref, terms)


def collect(here, index, base, inner, outer):
    terms, cells = base.shape
    smem = pl.BlockSpec(memory_space=pltpu.SMEM)
    vmem = pl.BlockSpec(memory_space=pltpu.VMEM)
    return pl.pallas_call(
        collect_kernel,
        out_shape=jax.ShapeDtypeStruct(base.shape, jnp.float32),
        in_specs=[smem] + [vmem] * (3 + len(outer)),
        out_specs=vmem,
        scratch_shapes=[
            pltpu.VMEM((len(outer) + 1 + 2 * REACH, terms, LANES), jnp.float32),
            pltpu.VMEM((cells // 2, 2 * LANES), jnp.float32),
        ],
        compiler_params=pltpu.CompilerParams(vmem_limit_bytes=SMALL_LIMIT),
    )(here, index, base, inner, *outer)


def exchange(inner, outer):
    count = len(outer) + 1
    outer = [
        lax.ppermute(block, "gx", [(p, (p + k + 1) % count) for p in range(count)]) for k, block in enumerate(outer)
    ]
    return lax.all_to_all(inner, "gy", split_axis=0, concat_axis=0, tiled=True), outer


def per_device(multipoles, trans, pair_target, pair_source, send_list):
    offset_count, term_count, _ = trans.shape
    outer_count = lax.axis_size("gx")
    inner_count = lax.axis_size("gy")
    here = jnp.stack([lax.axis_index("gx"), lax.axis_index("gy")]).astype(jnp.int32)
    inner, outer = exchange(*pack(here, send_list, multipoles, outer_count, inner_count))

    used = jnp.sum((pair_target >= 0).astype(jnp.int32), axis=1)
    grains = (used + (GRAIN - 1)) // GRAIN
    ends = jnp.cumsum(grains)
    starts = jnp.concatenate([jnp.zeros((1,), jnp.int32), ends]) * GRAIN
    grain_count = -(-pair_target.size // WIDTH) * (WIDTH // GRAIN) + 2 * WIDTH // GRAIN
    grain_index = jnp.arange(grain_count, dtype=jnp.int32)
    offsets = jnp.sum((ends[None, :] <= grain_index[:, None]).astype(jnp.int32), axis=1)
    offsets = jnp.minimum(offsets, offset_count - 1)

    sign = parity_signs(term_count)[:, None]
    own, inner_back, outer_back = translate(
        starts, offsets, here, pair_target, pair_source, trans, multipoles, sign, inner, outer
    )
    return collect(here, send_list, own, *exchange(inner_back, outer_back))


def solution(mesh):
    placed = (
        P(None, ("gx", "gy")),
        P(),
        P(None, ("gx", "gy")),
        P(None, ("gx", "gy")),
        P(("gx", "gy"), None),
    )
    return jax.shard_map(
        per_device, mesh=mesh, in_specs=placed, out_specs=P(None, ("gx", "gy")), check_vma=False
    )
```

```python
import functools

import jax
import jax.numpy as jnp
from jax import lax
from jax.experimental import pallas as pl
from jax.experimental.pallas import tpu as pltpu
from jax.sharding import PartitionSpec as P

REACH = 4
LANES = 128
SUBLANES = 16
WIDTH = 1024
GRAIN = 32
DIRECT = 2
FOLD = 256
SCRATCHES = 15
SHORT = 64
PACK_LIMIT = 60 * 1024 * 1024
VMEM_LIMIT = 53 * 1024 * 1024
SMALL_LIMIT = 16 * 1024 * 1024


def parity_signs(term_count):
    term_index = jnp.arange(term_count, dtype=jnp.int32)
    degree = (term_index >= 1).astype(jnp.int32) + (term_index >= 4).astype(jnp.int32)
    degree = degree + (term_index >= 10).astype(jnp.int32) + (term_index >= 20).astype(jnp.int32)
    degree = degree + (term_index >= 35).astype(jnp.int32)
    return jnp.where(degree % 2 == 0, 1.0, -1.0).astype(jnp.float32)


def hot_columns(places, size):
    count = places[0].shape[1]
    tall = (SUBLANES, count)
    one, none = jnp.ones((), jnp.bfloat16), jnp.zeros((), jnp.bfloat16)
    row = lax.broadcasted_iota(jnp.int32, tall, 0).astype(jnp.float32)
    rows = [(row + float(k)).astype(jnp.bfloat16) for k in range(0, size, SUBLANES)]
    blocks = []
    for place in places:
        wanted = jnp.broadcast_to(place.astype(jnp.float32), tall).astype(jnp.bfloat16)
        blocks += [jnp.where(one_row == wanted, one, none) for one_row in rows]
    return jnp.concatenate(blocks, axis=0)


def stack_parts(values):
    high = values.astype(jnp.bfloat16).astype(jnp.float32)
    return jnp.concatenate([high, values - high], axis=0).astype(jnp.bfloat16)


def scatter_product(index_row, half, parts):
    rows, count = parts.shape
    upper = jnp.broadcast_to(index_row >= half, (rows, count))
    none = jnp.zeros((), jnp.bfloat16)
    pad = jnp.zeros((LANES - rows, count), jnp.bfloat16)
    spread = jnp.concatenate([jnp.where(upper, none, parts), pad, jnp.where(upper, parts, none), pad], axis=0)
    place = jnp.where(index_row >= half, index_row - half, index_row)
    hot = hot_columns([place - j * LANES for j in range(half // LANES)], LANES)
    return lax.dot_general(
        hot, spread, (((1,), (1,)), ((), ())), preferred_element_type=jnp.float32
    )


def unfold(acc_ref, terms):
    sides = []
    for side in range(2):
        turned = acc_ref[:, side * LANES : (side + 1) * LANES].T
        sides.append(turned[:terms] + turned[terms : 2 * terms])
    return jnp.concatenate(sides, axis=1)


def pick(options, which):
    chosen = options[0]
    for k in range(1, len(options)):
        chosen = jnp.where(which == k, options[k], chosen)
    return chosen


def batch_of(count, most):
    return max(k for k in range(1, most + 1) if count % k == 0)


def compact(starts_ref, tables):
    offset_count, slot_count = tables[0][0].shape
    pieces = slot_count // LANES
    for _, out_ref in tables:
        out_ref[...] = jnp.full(out_ref.shape, -1, jnp.int32)
    lane = lax.broadcasted_iota(jnp.int32, (8, LANES), 1)
    empty = jnp.full((8, LANES), -1, jnp.int32)
    batch = batch_of(offset_count, 4)

    def place(step, kept):
        kept = list(kept)
        for u in range(batch):
            offset = step * batch + u
            start = starts_ref[offset]
            row, shift = start >> 7, start & (LANES - 1)
            crossed = (starts_ref[offset + 1] >> 7) - row
            inside = lane >= shift
            for k, (pairs_ref, out_ref) in enumerate(tables):
                line = pairs_ref[pl.ds(offset, 1), :]
                turned = [
                    pltpu.roll(jnp.broadcast_to(line[:, q * LANES : (q + 1) * LANES], (8, LANES)), shift, 1)
                    for q in range(pieces)
                ]
                turned = [kept[k], *turned, empty]
                tiles = [jnp.where(inside, turned[q + 1], turned[q]) for q in range(pieces + 1)]
                for q, tile in enumerate(tiles):
                    out_ref[pl.ds(row + q, 1), :] = tile[:1]
                kept[k] = pick(tiles, crossed)
        return tuple(kept)

    lax.fori_loop(0, offset_count // batch, place, (empty,) * len(tables))


def turn_matrices(t_ref, matrix_ref):
    terms, _, offset_count = t_ref.shape
    turns = batch_of(terms, 4)

    def turn(step, carry):
        for u in range(turns):
            i = step * turns + u
            parts = stack_parts(t_ref[i]).T.astype(jnp.float32)
            pad = jnp.zeros((offset_count, LANES - 2 * terms), jnp.float32)
            matrix_ref[pl.ds(i, offset_count, stride=terms), :] = jnp.concatenate([parts, pad], axis=1)
        return carry

    lax.fori_loop(0, terms // turns, turn, 0)


def index_row(ref, first, count):
    return jnp.concatenate([ref[pl.ds(first + q, 1), :] for q in range(count)], axis=1)


def gather_columns(parts, index):
    terms = parts[0].shape[0]
    lane = jnp.broadcast_to(index & (LANES - 1), (terms, LANES))
    chunk = jnp.broadcast_to(index >> 7, (8, LANES))
    picked = [jnp.zeros((8, LANES), jnp.float32)] * (terms // 8)
    for c, part in enumerate(parts):
        found = jnp.take_along_axis(part[...], lane, axis=1, mode="promise_in_bounds")
        here = chunk == c
        picked = [jnp.where(here, found[8 * r : 8 * r + 8], some) for r, some in enumerate(picked)]
    return jnp.concatenate(picked, axis=0)


def fold_columns(fold_ref, parts, index):
    count = index.shape[1]
    hot = hot_columns([index & (FOLD - 1)], FOLD)
    found = jnp.dot(fold_ref[...], hot, preferred_element_type=jnp.float32)
    chunk = jnp.broadcast_to(index >> (FOLD.bit_length() - 1), (8, count))
    masks = [chunk == c for c in range(fold_ref.shape[0] // parts)]
    picked = []
    for r in range(0, parts, 8):
        some = jnp.zeros((8, count), jnp.float32)
        for c, mask in enumerate(masks):
            some = jnp.where(mask, found[c * parts + r : c * parts + r + 8], some)
        picked.append(some)
    return jnp.concatenate(picked, axis=0)


def block_for(place, here, sign):
    distance = (place - here) * sign
    block = jnp.where(distance > 0, distance - 1, REACH - 1 - distance)
    there = (distance != 0) & (distance <= REACH) & (distance >= -REACH)
    return jnp.where(there, block, 0), there


def sender_of(block, here, sign, count):
    step = block + 1 if block < REACH else REACH - 1 - block
    place = here - step * sign
    return jnp.clip(place, 0, count - 1), (place >= 0) & (place < count)


def turned(place, count):
    return jnp.where(place >= count, place - count, jnp.where(place < 0, place + count, place))


def upper_blocks(here, count):
    return jnp.minimum(count - 1 - here, REACH)


def rank_of(block, here_ref, outer_count, inner_count):
    outer = block - jnp.where(block > here_ref[0], 1, 0)
    lower = block - 1 - REACH + upper_blocks(here_ref[1], inner_count)
    return jnp.where(block < outer_count, outer, jnp.where(block < outer_count + REACH, block - 1, lower))


def most_blocks(outer_count, inner_count):
    along = [min(REACH, inner_count - 1 - p) + min(REACH, p) for p in range(inner_count)]
    return outer_count - 1 + max(along)


def hand_out(read, here_ref, sign, outer_refs, inner_ref):
    outer_count = len(outer_refs) + 1
    for k, ref in enumerate(outer_refs):
        ref[...] = read(turned(here_ref[0] + k + 1, outer_count), True)

    def hand(place, carry):
        block, there = block_for(place, here_ref[1], sign)
        inner_ref[place] = read(outer_count + block, there)
        return carry

    lax.fori_loop(0, inner_ref.shape[0], hand, 0, unroll=4)


def take_in(put, here_ref, sign, outer_refs, inner_ref):
    outer_count = len(outer_refs) + 1
    for k, ref in enumerate(outer_refs):
        put(turned(here_ref[0] - k - 1, outer_count), True, ref[...])
    for block in range(2 * REACH):
        sender, there = sender_of(block, here_ref[1], sign, inner_ref.shape[0])
        put(outer_count + block, there, inner_ref[sender])


def translate_kernel(*refs):
    outer_count = (len(refs) - SCRATCHES - 11) // 2
    inputs, refs = refs[:9], refs[9:]
    outer_refs, refs = refs[:outer_count], refs[outer_count:]
    own_ref, inner_back_ref, refs = refs[0], refs[1], refs[2:]
    outer_back_refs, refs = refs[:outer_count], refs[outer_count:]
    translate_body(*inputs, outer_refs, own_ref, inner_back_ref, outer_back_refs, *refs)


def translate_body(
    starts_ref, offsets_ref, here_ref, pair_target_ref, pair_source_ref, trans_ref, multipoles_ref, sign_ref, inner_ref,
    outer_refs, own_ref, inner_back_ref, outer_back_refs,
    target_pairs_ref, source_pairs_ref, native_ref, x_ref, target_ref, source_ref, t_ref,
    fold_ref, signed_ref, near_ref, forward_ref, backward_ref, own_acc_ref, all_acc_ref, ready
):
    fetches = [
        pltpu.make_async_copy(here, there, ready.at[k])
        for k, (here, there) in enumerate(
            [
                (pair_target_ref, target_pairs_ref),
                (pair_source_ref, source_pairs_ref),
                (multipoles_ref, x_ref),
                (trans_ref, native_ref),
            ]
        )
    ]
    for fetch in fetches:
        fetch.start()
    terms, cells = x_ref.shape
    outer_count, inner_count = len(outer_refs) + 1, inner_ref.shape[0]
    spare = near_ref.shape[0] - 1
    chunks = cells // LANES
    own_half = cells // 2
    all_half = all_acc_ref.shape[0]
    parts = 2 * terms
    per_step = WIDTH // LANES
    grains = LANES // GRAIN

    for fetch in fetches[:3]:
        fetch.wait()
    folds = cells // FOLD
    signed_ref[...] = x_ref[...] * sign_ref[...]
    for c in range(folds):
        fold_ref[c * parts : (c + 1) * parts, :] = stack_parts(signed_ref[:, c * FOLD : (c + 1) * FOLD])
    near_ref[...] = jnp.zeros_like(near_ref)

    def put(block, there, value):
        near_ref[jnp.where(there, rank_of(block, here_ref, outer_count, inner_count), spare)] = value

    take_in(put, here_ref, -1, outer_refs, inner_ref)
    own_acc_ref[...] = jnp.zeros_like(own_acc_ref)
    all_acc_ref[...] = jnp.zeros_like(all_acc_ref)
    forward_ref[...] = jnp.zeros_like(forward_ref)
    backward_ref[...] = jnp.zeros_like(backward_ref)

    def own_columns(ref):
        return [ref.at[:, c * LANES : (c + 1) * LANES] for c in range(chunks)]

    compact(starts_ref, [(target_pairs_ref, target_ref), (source_pairs_ref, source_ref)])
    position = source_ref[...]
    absent = REACH - upper_blocks(here_ref[1], inner_count)
    after_self = position >= cells + (here_ref[0] + 1) * LANES
    after_upper = position >= cells + (outer_count + REACH) * LANES
    source_ref[...] = position - jnp.where(after_self, LANES, 0) - jnp.where(after_upper, absent * LANES, 0)
    fetches[3].wait()
    turn_matrices(native_ref, t_ref)
    steps = (starts_ref[starts_ref.shape[0] - 1] + (WIDTH - 1)) // WIDTH
    low_lanes = lax.broadcasted_iota(jnp.int32, (terms, 2 * LANES), 1) & (LANES - 1)

    def scatter(group):
        first = jnp.maximum(group, 0) * per_step
        own_acc_ref[...] += scatter_product(index_row(target_ref, first, per_step), own_half, forward_ref[...])
        all_acc_ref[...] += scatter_product(index_row(source_ref, first, per_step), all_half, backward_ref[...])

    def step(group, carry):
        scatter(group - 1)
        ahead, back = [], []
        targets = fold_columns(fold_ref, parts, index_row(target_ref, group * per_step + DIRECT, per_step - DIRECT))
        for q in range(per_step):
            row = group * per_step + q
            sources = gather_columns(
                own_columns(x_ref) + [near_ref.at[k] for k in range(spare)], source_ref[pl.ds(row, 1), :]
            )
            if q < DIRECT:
                direct = gather_columns(own_columns(signed_ref), target_ref[pl.ds(row, 1), :])
                both = jnp.concatenate([sources, direct], axis=1)
                high = both.astype(jnp.bfloat16).astype(jnp.float32)
                low = both - high
            else:
                here = slice((q - DIRECT) * LANES, (q - DIRECT + 1) * LANES)
                source_high = sources.astype(jnp.bfloat16).astype(jnp.float32)
                high = jnp.concatenate([source_high, targets[:terms, here]], axis=1)
                low = jnp.concatenate([sources - source_high, targets[terms:, here]], axis=1)
            gap = jnp.zeros((LANES - parts, 2 * LANES), jnp.float32)
            rest = jnp.zeros((SHORT - terms, 2 * LANES), jnp.float32)
            columns = jnp.concatenate([high, high, gap, low, rest], axis=0).astype(jnp.bfloat16)
            matrices = [
                t_ref[pl.ds(pl.multiple_of(offsets_ref[row * grains + g] * terms, 8), terms), :] for g in range(grains)
            ]
            matrices = jnp.concatenate(matrices, axis=0).astype(jnp.bfloat16)
            matrices = jnp.concatenate([matrices, matrices[:, :SHORT]], axis=1)
            moved = jnp.dot(matrices, columns, preferred_element_type=jnp.float32)
            total = moved[:terms]
            for g in range(1, grains):
                total = jnp.where(low_lanes >= g * GRAIN, moved[g * terms : (g + 1) * terms], total)
            total = stack_parts(total)
            ahead.append(total[:, :LANES])
            back.append(total[:, LANES:])
        for q in range(per_step):
            forward_ref[:, q * LANES : (q + 1) * LANES] = ahead[q]
            backward_ref[:, q * LANES : (q + 1) * LANES] = back[q]
        return carry

    lax.fori_loop(0, steps, step, 0)
    scatter(steps - 1)
    everywhere = unfold(all_acc_ref, terms) * sign_ref[...]
    own_ref[...] = unfold(own_acc_ref, terms) + everywhere[:, :cells]
    for k in range(spare):
        near_ref[k] = everywhere[:, cells + k * LANES : cells + (k + 1) * LANES]
    near_ref[spare] = jnp.zeros((terms, LANES), jnp.float32)

    def read(block, there):
        return near_ref[jnp.where(there, rank_of(block, here_ref, outer_count, inner_count), spare)]

    hand_out(read, here_ref, 1, outer_back_refs, inner_back_ref)


def translate(starts, offsets, here, pair_target, pair_source, trans, x, sign, inner, outer):
    terms, cells = x.shape
    offset_count = pair_target.shape[0]
    row_count = offsets.shape[0] * GRAIN // LANES
    hbm = pl.BlockSpec(memory_space=pltpu.HBM)
    outer_count = len(outer)
    near_count = most_blocks(outer_count + 1, inner.shape[0])
    own_half = cells // 2
    all_half = -(-(cells + near_count * LANES) // (2 * LANES)) * LANES
    smem = pl.BlockSpec(memory_space=pltpu.SMEM)
    vmem = pl.BlockSpec(memory_space=pltpu.VMEM)
    own, inner_back, *outer_back = pl.pallas_call(
        translate_kernel,
        out_shape=[jax.ShapeDtypeStruct(like.shape, jnp.float32) for like in (x, inner, *outer)],
        in_specs=[smem] * 3 + [hbm] * 4 + [vmem] * (2 + outer_count),
        out_specs=[vmem] * (2 + outer_count),
        scratch_shapes=[
            pltpu.VMEM(pair_target.shape, jnp.int32),
            pltpu.VMEM(pair_source.shape, jnp.int32),
            pltpu.VMEM((terms, terms, offset_count), jnp.float32),
            pltpu.VMEM((terms, cells), jnp.float32),
            pltpu.VMEM((row_count, LANES), jnp.int32),
            pltpu.VMEM((row_count, LANES), jnp.int32),
            pltpu.VMEM((offset_count * terms, LANES), jnp.float32),
            pltpu.VMEM((2 * terms * (cells // FOLD), FOLD), jnp.bfloat16),
            pltpu.VMEM((terms, cells), jnp.float32),
            pltpu.VMEM((near_count + 1, terms, LANES), jnp.float32),
            pltpu.VMEM((2 * terms, WIDTH), jnp.bfloat16),
            pltpu.VMEM((2 * terms, WIDTH), jnp.bfloat16),
            pltpu.VMEM((own_half, 2 * LANES), jnp.float32),
            pltpu.VMEM((all_half, 2 * LANES), jnp.float32),
            pltpu.SemaphoreType.DMA((4,)),
        ],
        compiler_params=pltpu.CompilerParams(vmem_limit_bytes=VMEM_LIMIT),
        cost_estimate=pl.CostEstimate(flops=100_000_000_000, bytes_accessed=12_000_000, transcendentals=0),
    )(starts, offsets, here, pair_target, pair_source, trans.transpose(1, 2, 0), x, sign, inner, *outer)
    return own, inner_back, outer_back


def pack_kernel(here_ref, send_ref, multipoles_ref, inner_ref, *refs):
    outer_refs, (index_ref, x_ref, ready) = refs[:-3], refs[-3:]
    cells = x_ref.shape[1]
    fetches = [
        pltpu.make_async_copy(send_ref, index_ref, ready.at[0]),
        pltpu.make_async_copy(multipoles_ref, x_ref, ready.at[1]),
    ]
    for fetch in fetches:
        fetch.start()
    for fetch in fetches:
        fetch.wait()

    def read(block, there):
        index = index_ref[:, pl.ds(pl.multiple_of(block * LANES, LANES), LANES)]
        index = index if there is True else jnp.where(there, index, -1)
        return gather_columns([x_ref.at[:, c * LANES : (c + 1) * LANES] for c in range(cells // LANES)], index)

    hand_out(read, here_ref, -1, outer_refs, inner_ref)


def pack(here, index, x, outer_count, inner_count):
    smem = pl.BlockSpec(memory_space=pltpu.SMEM)
    vmem = pl.BlockSpec(memory_space=pltpu.VMEM)
    hbm = pl.BlockSpec(memory_space=pltpu.HBM)
    block = (x.shape[0], LANES)
    inner, *outer = pl.pallas_call(
        pack_kernel,
        out_shape=[jax.ShapeDtypeStruct((inner_count, *block), jnp.float32)]
        + [jax.ShapeDtypeStruct(block, jnp.float32)] * (outer_count - 1),
        in_specs=[smem, hbm, hbm],
        out_specs=[vmem] * outer_count,
        scratch_shapes=[
            pltpu.VMEM(index.shape, jnp.int32),
            pltpu.VMEM(x.shape, jnp.float32),
            pltpu.SemaphoreType.DMA((2,)),
        ],
        compiler_params=pltpu.CompilerParams(vmem_limit_bytes=PACK_LIMIT),
    )(here, index, x)
    return inner, outer


def collect_kernel(here_ref, index_ref, base_ref, inner_ref, *refs):
    outer_refs, (out_ref, near_ref, acc_ref) = refs[:-3], refs[-3:]
    terms, cells = base_ref.shape
    half = cells // 2
    near_ref[here_ref[0]] = jnp.zeros((terms, LANES), jnp.float32)

    def put(block, there, value):
        near_ref[block] = jnp.where(there, value, 0.0)

    take_in(put, here_ref, 1, outer_refs, inner_ref)
    parts = stack_parts(jnp.concatenate([near_ref[k] for k in range(near_ref.shape[0])], axis=1))
    acc_ref[...] = scatter_product(index_ref[...], half, parts)
    out_ref[...] = base_ref[...] + unfold(acc_ref, terms)


def collect(here, index, base, inner, outer):
    terms, cells = base.shape
    smem = pl.BlockSpec(memory_space=pltpu.SMEM)
    vmem = pl.BlockSpec(memory_space=pltpu.VMEM)
    return pl.pallas_call(
        collect_kernel,
        out_shape=jax.ShapeDtypeStruct(base.shape, jnp.float32),
        in_specs=[smem] + [vmem] * (3 + len(outer)),
        out_specs=vmem,
        scratch_shapes=[
            pltpu.VMEM((len(outer) + 1 + 2 * REACH, terms, LANES), jnp.float32),
            pltpu.VMEM((cells // 2, 2 * LANES), jnp.float32),
        ],
        compiler_params=pltpu.CompilerParams(vmem_limit_bytes=SMALL_LIMIT),
    )(here, index, base, inner, *outer)


def exchange(inner, outer):
    count = len(outer) + 1
    outer = [
        lax.ppermute(block, "gx", [(p, (p + k + 1) % count) for p in range(count)]) for k, block in enumerate(outer)
    ]
    return lax.all_to_all(inner, "gy", split_axis=0, concat_axis=0, tiled=True), outer


def per_device(multipoles, trans, pair_target, pair_source, send_list):
    offset_count, term_count, _ = trans.shape
    outer_count = lax.axis_size("gx")
    inner_count = lax.axis_size("gy")
    here = jnp.stack([lax.axis_index("gx"), lax.axis_index("gy")]).astype(jnp.int32)
    inner, outer = exchange(*pack(here, send_list, multipoles, outer_count, inner_count))

    used = jnp.sum((pair_target >= 0).astype(jnp.int32), axis=1)
    grains = (used + (GRAIN - 1)) // GRAIN
    ends = jnp.cumsum(grains)
    starts = jnp.concatenate([jnp.zeros((1,), jnp.int32), ends]) * GRAIN
    grain_count = -(-pair_target.size // WIDTH) * (WIDTH // GRAIN) + 2 * WIDTH // GRAIN
    grain_index = jnp.arange(grain_count, dtype=jnp.int32)
    offsets = jnp.sum((ends[None, :] <= grain_index[:, None]).astype(jnp.int32), axis=1)
    offsets = jnp.minimum(offsets, offset_count - 1)

    sign = parity_signs(term_count)[:, None]
    own, inner_back, outer_back = translate(
        starts, offsets, here, pair_target, pair_source, trans, multipoles, sign, inner, outer
    )
    return collect(here, send_list, own, *exchange(inner_back, outer_back))


def solution(mesh):
    placed = (
        P(None, ("gx", "gy")),
        P(),
        P(None, ("gx", "gy")),
        P(None, ("gx", "gy")),
        P(("gx", "gy"), None),
    )
    return jax.shard_map(
        per_device, mesh=mesh, in_specs=placed, out_specs=P(None, ("gx", "gy")), check_vma=False
    )
```
